32 devices in a mesh: leaf: 32 (over z, y, x, core).
Axes of the slice: x: 2, y: 2, z: 4, core: 2. Of those that a mesh axis runs over, the one named last changes fastest.
Arguments:
- coords: float32 [6, 262144], P(None, 'leaf'), may hold values from 0 to 4
- right_sides: float32 [8, 262144], P(None, 'leaf'), may hold values from -6 to 6
- projection: float32 [262144, 256], P('leaf'), may hold values from -0.0625 to 0.0625
- skel_index: int32 [32, 256], P('leaf'), may hold values from 0 to 8191
- selection: int32 [30, 256], replicated, may hold values from 0 to 511
- transfer: float32 [512, 256], replicated, may hold values from -0.25 to 0.25
- near_leaf: int32 [1024, 8], P('leaf'), may hold values from 0 to 1023, as said below
- near_count: int32 [1024], P('leaf'), may hold values from 1 to 8, as said below
Outputs:
- product: float32 [8, 262144], P(None, 'leaf')
The draws below stay inside these ranges and needn't reach their ends.
Inputs may be any that keep to these rules, and one draw needn't show every extreme that they name: `near_leaf`: slot 0 of leaf g is g itself; every listed leaf is held by the device subtree of g or by one of the two subtrees next to it. `near_count`: all leaves of some device subtrees use all 8 slots; the others use up to 4.
All inputs are finite; a program needn't handle non-finite values.
Results may differ from the reference program's by a relative error of at most 0.0003.
Values sent between devices are 32-bit elements; how exact they have to be, the bound alone decides.
No kernel may reach another device: no remote copies, remote signals or barrier semaphores. Data moves between devices by JAX's collectives and lax.ppermute only.
A program may use at most 192 MiB of HBM per device.

```python
import jax
import jax.numpy as jnp
from jax import lax

DIMS = 6
RHS = 8
LEAF = 256
RANK = 256
NEAR = 8
LEAVES_DEV = 32
PTS_DEV = 8192
LEAVES = 1024
POINTS = 262144
LEVELS = 5
N_LEAF = 32


def draw_coords(key, part):
    key = jax.random.fold_in(key, 11)
    noise = jnp.clip(1.25 + 0.6 * jax.random.normal(key, (DIMS, POINTS), jnp.float32), 0.0, 2.5)
    device = jnp.arange(POINTS, dtype=jnp.int32) // PTS_DEV
    offsets = jnp.zeros((DIMS, POINTS), jnp.float32)
    rows = jnp.arange(DIMS, dtype=jnp.int32)
    for level in range(8):
        bit_on = (device // 2 ** level % 2).astype(jnp.float32)
        offsets = offsets + 0.6 * (rows[:, None] == level % DIMS).astype(jnp.float32) * bit_on[None, :]
    return noise + offsets


def draw_near_leaf(key, part):
    key = jax.random.fold_in(key, 23)
    key_side, key_local = jax.random.split(key)
    leaves = jnp.arange(LEAVES, dtype=jnp.int32)
    device = leaves // LEAVES_DEV
    side = jax.random.randint(key_side, (LEAVES, NEAR), -1, 2)
    owner = jnp.clip(device[:, None] + side, 0, N_LEAF - 1)
    local = jax.random.randint(key_local, (LEAVES, NEAR), 0, LEAVES_DEV)
    chosen = owner * LEAVES_DEV + local
    first = jnp.arange(NEAR, dtype=jnp.int32)[None, :] == 0
    return jnp.where(first, leaves[:, None], chosen).astype(jnp.int32)


def draw_near_count(key, part):
    key = jax.random.fold_in(key, 37)
    key_heavy, key_light = jax.random.split(key)
    device = jnp.arange(LEAVES, dtype=jnp.int32) // LEAVES_DEV
    heavy_dev = jax.random.randint(key_heavy, (N_LEAF,), 0, 4) == 0
    heavy_dev = heavy_dev | (jnp.arange(N_LEAF, dtype=jnp.int32) == 0)
    light = jax.random.randint(key_light, (LEAVES,), 1, NEAR // 2 + 1)
    return jnp.where(heavy_dev[device], NEAR, light).astype(jnp.int32)


def plant(result, stream_key, smallest, largest):
    place = [jax.random.randint(jax.random.fold_in(stream_key, axis), (), 0, length) for axis, length in enumerate(result.shape)]
    longest = result.shape.index(max(result.shape))
    next_to = place[:longest] + [(place[longest] + 1) % result.shape[longest]] + place[longest + 1:]
    return result.at[tuple(place)].set(smallest).at[tuple(next_to)].set(largest)


def shard_levels(rng, dims, shards, smallest, high):
    gain = 1.0
    for axis_at, shards_of in shards:
        draws = jax.random.uniform(jax.random.fold_in(jax.random.fold_in(rng, 6), axis_at), (shards_of,), jnp.float32, smallest / len(shards), high / len(shards))
        gain = gain * jnp.repeat(jnp.exp(draws), dims[axis_at] // shards_of).reshape((-1,) + (1,) * (len(dims) - 1 - axis_at))
    return gain


def bell_draw(own_key, shape, spread, most, shards=(), kind=jnp.bfloat16):
    values = jax.random.normal(own_key, shape, jnp.float32) * spread
    if len(shards) > 0:
        values = shard_levels(own_key, shape, shards, -0.22, 0.18) * values
    return jnp.clip(values, min=-most, max=most).astype(kind)


def setup_inputs(seed: int = 0) -> dict:
    seeds = jax.random.split(jax.random.key(seed), 9)
    coords = draw_coords(jax.random.fold_in(seeds[8], 71), 0)
    right_sides = bell_draw(seeds[1], (RHS, POINTS), 1.0, 6.0, ((1, 32),), jnp.float32)
    projection = bell_draw(seeds[2], (POINTS, RANK), PTS_DEV ** -0.5, 0.0625, ((0, 32),), jnp.float32)
    skel_index = plant(jax.random.randint(seeds[3], (N_LEAF, RANK), 0, PTS_DEV), jax.random.fold_in(seeds[3], 1), 0, PTS_DEV - 1).astype(jnp.int32)
    selection = plant(jax.random.randint(seeds[4], (N_LEAF - 2, RANK), 0, 2 * RANK), jax.random.fold_in(seeds[4], 1), 0, (2 * RANK) - 1).astype(jnp.int32)
    transfer = bell_draw(seeds[5], (2 * RANK, RANK), (2 * RANK) ** -0.5, 0.25, (), jnp.float32)
    near_leaf = draw_near_leaf(jax.random.fold_in(seeds[8], 71), 0)
    near_count = draw_near_count(jax.random.fold_in(seeds[8], 71), 0)
    return {"coords": coords, "right_sides": right_sides, "projection": projection, "skel_index": skel_index, "selection": selection, "transfer": transfer, "near_leaf": near_leaf, "near_count": near_count}


def kernel_block(sources, targets):
    dots = lax.dot_general(sources, targets, (((0,), (0,)), ((), ())), precision=lax.Precision.HIGHEST)
    src_sq = jnp.sum(sources * sources, axis=0)
    tgt_sq = jnp.sum(targets * targets, axis=0)
    distance = jnp.maximum(src_sq[:, None] + tgt_sq[None, :] - 2.0 * dots, 0.0)
    return jnp.exp(-0.5 * distance)


def reference(coords, right_sides, projection, skel_index, selection, transfer, near_leaf, near_count):
    leaf_coords = jnp.moveaxis(coords.reshape(DIMS, LEAVES, LEAF), 1, 0)
    leaf_values = jnp.moveaxis(right_sides.reshape(RHS, LEAVES, LEAF), 1, 0)

    def near_one(inputs):
        targets, sources_list, count = inputs

        def slot_term(source_leaf, slot):
            src_c = leaf_coords[source_leaf]
            src_x = leaf_values[source_leaf]
            block = kernel_block(src_c, targets)
            term = jnp.dot(src_x, block, precision=lax.Precision.HIGHEST)
            return jnp.where(slot < count, term, jnp.zeros_like(term))

        slots = jnp.arange(NEAR, dtype=jnp.int32)
        return jnp.sum(jax.vmap(slot_term)(sources_list, slots), axis=0)

    near = lax.map(near_one, (leaf_coords, near_leaf, near_count))
    near = jnp.moveaxis(near, 0, 1).reshape(RHS, POINTS)

    dev_coords = jnp.moveaxis(coords.reshape(DIMS, N_LEAF, PTS_DEV), 1, 0)
    dev_values = jnp.moveaxis(right_sides.reshape(RHS, N_LEAF, PTS_DEV), 1, 0)
    dev_proj = projection.reshape(N_LEAF, PTS_DEV, RANK)
    level_w = jnp.einsum("nrp,npk->nrk", dev_values, dev_proj, precision=lax.Precision.HIGHEST)
    level_c = jnp.take_along_axis(dev_coords, skel_index[:, None, :], axis=2)
    far = jnp.zeros((N_LEAF, RHS, PTS_DEV), jnp.float32)
    devices = jnp.arange(N_LEAF, dtype=jnp.int32)
    for level in range(LEVELS):
        def far_one(inputs):
            device, targets = inputs
            partner = jnp.bitwise_xor(device // (2 ** level), 1)
            far_c = level_c[partner]
            far_w = level_w[partner]
            return jnp.dot(far_w, kernel_block(far_c, targets), precision=lax.Precision.HIGHEST)

        far = far + lax.map(far_one, (devices, dev_coords))
        if level < LEVELS - 1:
            count = N_LEAF // (2 ** (level + 1))
            offset = N_LEAF - N_LEAF // (2 ** level)
            pair_c = level_c.reshape(count, 2, DIMS, RANK)
            pair_w = level_w.reshape(count, 2, RHS, RANK)
            joined_c = jnp.concatenate([pair_c[:, 0], pair_c[:, 1]], axis=2)
            joined_w = jnp.concatenate([pair_w[:, 0], pair_w[:, 1]], axis=2)
            picked = selection[offset:offset + count]
            level_c = jnp.take_along_axis(joined_c, picked[:, None, :], axis=2)
            level_w = jnp.einsum("nrj,jk->nrk", joined_w, transfer, precision=lax.Precision.HIGHEST)
    far = jnp.moveaxis(far, 0, 1).reshape(RHS, POINTS)
    return (near + far) * (1.0 / (NEAR * LEAF) ** 0.5)
```

```python
import functools
import math

import jax
import jax.numpy as jnp
from jax import lax
from jax.experimental import pallas as pl
from jax.experimental.pallas import tpu as pltpu
from jax.sharding import PartitionSpec as P

F32 = jnp.float32
BF16 = jnp.bfloat16
LANES = 128
SHIFT = 2.0
LEAVES_TURN = 4
LEAVES_SELF = 8
ROOT = math.sqrt(math.log2(math.e))
SMEM_SPEC = pl.BlockSpec(memory_space=pltpu.SMEM)
HBM_SPEC = pl.BlockSpec(memory_space=pltpu.HBM)
VMEM_SPEC = pl.BlockSpec(memory_space=pltpu.VMEM)


def swap(value, axis, first):
    count = lax.axis_size(axis)
    pairs = []
    for left in range(first, count - 1, 2):
        pairs += [(left, left + 1), (left + 1, left)]
    return lax.ppermute(value, axis, pairs)


def two_pieces(value):
    high = value.astype(BF16).astype(F32)
    return high, value - high


def three_pieces(value):
    high, rest = two_pieces(value)
    middle, low = two_pieces(rest)
    return high, middle, low


def source_form(extended):
    high, middle, low = three_pieces(extended)
    return jnp.concatenate([high, high, high, middle, middle, low], axis=0).astype(BF16)


def target_form(extended):
    row = lax.broadcasted_iota(jnp.int32, extended.shape, 0)
    below = pltpu.roll(extended, 1, 0)
    swapped = jnp.where(row == 6, 1.0, jnp.where(row == 7, below, extended))
    high, middle, low = three_pieces(swapped)
    return jnp.concatenate([high, middle, low, high, middle, high], axis=0).astype(BF16)


def weight_form(values):
    high, low = two_pieces(values)
    return jnp.concatenate([high, low], axis=0).astype(BF16)


def pick_columns(pieces, index):
    index = jnp.broadcast_to(index, (8, LANES))
    low = index & (LANES - 1)
    high = index >> 7
    result = jnp.take_along_axis(pieces[0], low, axis=1)
    for at in range(1, len(pieces)):
        result = jnp.where(high == at, jnp.take_along_axis(pieces[at], low, axis=1), result)
    return result


def split_block(exponent):
    kernel = jnp.exp2(exponent)
    high = jnp.minimum(kernel.astype(BF16), jnp.ones((), BF16))
    return high, (kernel - high.astype(F32)).astype(BF16)


def kernel_term(source, target, weight, rows):
    highs, lows = [], []
    for first in range(0, source.shape[0], rows):
        high, low = split_block(jnp.dot(source[first:first + rows], target, preferred_element_type=F32))
        highs.append(high)
        lows.append(low)
    high = jnp.concatenate(highs, axis=0) if len(highs) > 1 else highs[0]
    low = jnp.concatenate(lows, axis=0) if len(lows) > 1 else lows[0]
    both = jnp.dot(weight, high, preferred_element_type=F32)
    return both + jnp.dot(weight, low, preferred_element_type=F32)


def fold(pieces):
    return pieces[:8] + pieces[8:]


def extend_kernel(coords_ref, right_ref, index_hbm, out_ref, index_ref, held, sems):
    rows, points = held.shape
    copies = [
        pltpu.make_async_copy(coords_ref, held, sems.at[0]),
        pltpu.make_async_copy(right_ref, out_ref.at[pl.ds(8, 8)], sems.at[1]),
        pltpu.make_async_copy(index_hbm, index_ref, sems.at[2]),
    ]
    for copy in copies:
        copy.start()
    copies[0].wait()
    centred = (held[...] - SHIFT) * ROOT
    out_ref[0:rows, :] = centred
    out_ref[rows:rows + 1, :] = -0.5 * jnp.sum(centred * centred, axis=0, keepdims=True)
    out_ref[rows + 1:rows + 2, :] = jnp.ones((1, points), F32)
    copies[1].wait()
    copies[2].wait()


def extend(coords, right_sides, skel_index):
    rows, points = coords.shape
    return pl.pallas_call(
        extend_kernel,
        out_shape=(pltpu.VMEM((16, points), F32), pltpu.VMEM(skel_index.shape, jnp.int32)),
        in_specs=[HBM_SPEC] * 3,
        out_specs=(VMEM_SPEC, VMEM_SPEC),
        scratch_shapes=[pltpu.VMEM((rows, points), F32), pltpu.SemaphoreType.DMA((3,))],
        compiler_params=pltpu.CompilerParams(vmem_limit_bytes=58 * 2**20),
        name="extend",
    )(coords, right_sides, skel_index)


def first_kernel(leaf, x_ref, proj_ref, index_ref, node_ref, self_ref, held, sources, weights, targets, sems):
    chunks = held.shape[0]
    chunk, rank = held.shape[1:]
    points = x_ref.shape[1]
    copies = [
        pltpu.make_async_copy(proj_ref.at[pl.ds(at * chunk, chunk)], held.at[at], sems.at[at]) for at in range(chunks)
    ]
    for copy in copies:
        copy.start()
    for half in range(rank // LANES):
        lanes = slice(half * LANES, (half + 1) * LANES)
        pieces = [x_ref[0:8, at * LANES:(at + 1) * LANES] for at in range(points // LANES)]
        columns = pick_columns(pieces, index_ref[:, lanes])
        for copy in range(node_ref.shape[0]):
            node_ref[copy, 0:8, lanes] = columns
    wide = 4 * leaf

    def prepare(at, _):
        columns = pl.ds(pl.multiple_of(at * wide, wide), wide)
        sources[:, columns] = source_form(x_ref[0:8, columns])
        weights[:, columns] = weight_form(x_ref[8:16, columns])
        targets[:, columns] = target_form(x_ref[0:8, columns])
        return 0

    def turn(at, _):
        for part in range(LEAVES_SELF):
            columns = pl.ds(pl.multiple_of((at * LEAVES_SELF + part) * leaf, leaf), leaf)
            self_ref[:, columns] = fold(kernel_term(sources[:, columns].T, targets[:, columns], weights[:, columns], 128))
        return 0

    lax.fori_loop(0, points // wide, prepare, 0)
    lax.fori_loop(0, points // (leaf * LEAVES_SELF), turn, 0)
    total = jnp.zeros((8, rank), F32)
    for at in range(chunks):
        x_high, x_low = two_pieces(x_ref[8:16, at * chunk:(at + 1) * chunk])
        left = jnp.concatenate([x_high, x_low], axis=0).astype(BF16)
        copies[at].wait()
        p_high, p_low = two_pieces(held[at])
        both = jnp.dot(left, p_high.astype(BF16), preferred_element_type=F32)
        part = jnp.dot(left, p_low.astype(BF16), preferred_element_type=F32)
        total += both[:8] + both[8:] + part[:8]
    for copy in range(node_ref.shape[0]):
        node_ref[copy, 8:16, :] = total


def first_step(copies, leaf, extended, projection, skel_index):
    points, rank = projection.shape
    chunks = 8
    return pl.pallas_call(
        functools.partial(first_kernel, leaf),
        out_shape=(
            jax.ShapeDtypeStruct((copies, 16, rank), F32),
            jax.ShapeDtypeStruct((8, points), F32),
        ),
        in_specs=[VMEM_SPEC, HBM_SPEC, VMEM_SPEC],
        out_specs=(VMEM_SPEC, VMEM_SPEC),
        scratch_shapes=[
            pltpu.VMEM((chunks, points // chunks, rank), F32),
            pltpu.VMEM((48, points), BF16),
            pltpu.VMEM((16, points), BF16),
            pltpu.VMEM((48, points), BF16),
            pltpu.SemaphoreType.DMA((chunks,)),
        ],
        compiler_params=pltpu.CompilerParams(vmem_limit_bytes=50 * 2**20),
        name="first_step",
    )(extended, projection, skel_index)


def climb(source, first, count, selection, rows, transfer, target, offset):
    rank = transfer[0].shape[1]
    t_high, t_low = transfer
    joined = jnp.concatenate(
        [
            jnp.concatenate([source[first + 2 * m + side, 8:16, :] for m in range(count)], axis=0)
            for side in range(2)
        ],
        axis=1,
    )
    high, low = two_pieces(joined)
    left = jnp.concatenate([high, low], axis=0).astype(BF16)
    both = jnp.dot(left, t_high, preferred_element_type=F32)
    part = jnp.dot(left, t_low, preferred_element_type=F32)
    moved = both[:8 * count] + both[8 * count:] + part[:8 * count]
    for m in range(count):
        target[offset + m, 8:16, :] = moved[m * 8:(m + 1) * 8, :]
        pieces = [
            source[first + 2 * m + side, 0:8, at * LANES:(at + 1) * LANES]
            for side in range(2)
            for at in range(rank // LANES)
        ]
        picked = selection[pl.ds(rows + m, 1), :]
        for half in range(rank // LANES):
            lanes = slice(half * LANES, (half + 1) * LANES)
            target[offset + m, 0:8, lanes] = pick_columns(pieces, picked[:, lanes])


def split_transfer(transfer_ref):
    t_high, t_low = two_pieces(transfer_ref[...])
    return t_high.astype(BF16), t_low.astype(BF16)


def near_kernel(near_ref, count_ref, self_ref, chip_ref, own_ref, other_ref, out_ref, sources, weights, targets):
    leaves, slots = near_ref.shape
    points = own_ref.shape[1]
    leaf = points // leaves
    own_index = lax.axis_index("leaf")
    even = own_index % 2 == 0
    first_leaf = own_index * leaves
    wide = 4 * leaf

    def prepare(at, _):
        columns = pl.ds(pl.multiple_of(at * wide, wide), wide)
        for part, ref in enumerate((chip_ref, own_ref, other_ref)):
            window = pl.ds(pl.multiple_of(part * points + at * wide, wide), wide)
            sources[:, window] = source_form(ref[0:8, columns])
            weights[:, window] = weight_form(ref[8:16, columns])
        targets[:, columns] = target_form(own_ref[0:8, columns])
        return 0

    lax.fori_loop(0, points // wide, prepare, 0)

    def window_place(offset):
        below, above = offset < 0, offset >= leaves
        left = jnp.where(even, 2, 0)
        part = jnp.where(below, left, jnp.where(above, 2 - left, 1))
        local = jnp.where(below, offset + leaves, jnp.where(above, offset - leaves, offset))
        return part * leaves + jnp.clip(local, 0, leaves - 1)

    def one_leaf(at, live_slots):
        columns = pl.ds(pl.multiple_of(at * leaf, leaf), leaf)
        target = targets[:, columns]
        total = jnp.zeros((16, leaf), F32)
        for slot in range(1, live_slots):
            place = window_place(near_ref[at, slot] - first_leaf)
            window = pl.ds(pl.multiple_of(place * leaf, leaf), leaf)
            weight = weights[:, window]
            weight = jnp.where(slot < count_ref[at], weight, jnp.zeros_like(weight))
            total += kernel_term(sources[:, window].T, target, weight, 128)
        out_ref[:, columns] = self_ref[:, columns] + fold(total)

    def turn(at, _):
        most = count_ref[LEAVES_TURN * at]
        for leaf_at in range(1, LEAVES_TURN):
            most = jnp.maximum(most, count_ref[LEAVES_TURN * at + leaf_at])
        heavy = most > slots // 2

        @pl.when(heavy)
        def _():
            for leaf_at in range(LEAVES_TURN):
                one_leaf(LEAVES_TURN * at + leaf_at, slots)

        @pl.when(jnp.logical_not(heavy))
        def _():
            for leaf_at in range(LEAVES_TURN):
                one_leaf(LEAVES_TURN * at + leaf_at, slots // 2)

        return 0

    lax.fori_loop(0, leaves // LEAVES_TURN, turn, 0)


def near_term(near_leaf, near_count, own_part, chip, own, other):
    leaves, slots = near_leaf.shape
    points = own.shape[1]
    entries = leaves * slots * (points // leaves) ** 2
    return pl.pallas_call(
        near_kernel,
        out_shape=jax.ShapeDtypeStruct((8, points), F32),
        in_specs=[SMEM_SPEC] * 2 + [VMEM_SPEC] * 4,
        out_specs=VMEM_SPEC,
        scratch_shapes=[
            pltpu.VMEM((48, 3 * points), BF16),
            pltpu.VMEM((16, 3 * points), BF16),
            pltpu.VMEM((48, points), BF16),
        ],
        cost_estimate=pl.CostEstimate(flops=1000 * entries, bytes_accessed=4 * 64 * points, transcendentals=entries),
        compiler_params=pltpu.CompilerParams(vmem_limit_bytes=32 * 2**20),
        name="near_term",
    )(near_leaf, near_count, own_part, chip, own, other)


def far_kernel(scale, tile, own_ref, near_ref, gathered_ref, selection_ref, transfer_ref, out_ref, nodes, sources, weights):
    devices = gathered_ref.shape[0]
    levels = devices.bit_length() - 1
    own_index = lax.axis_index("leaf")
    transfer = split_transfer(transfer_ref)
    rank = transfer_ref.shape[1]
    held, first = gathered_ref, 0
    for level in range(levels):
        node = held[first + ((own_index >> level) ^ 1)]
        form = source_form(node[0:8])
        sources[level] = jnp.concatenate([form, jnp.zeros((LANES - 48, rank), BF16)], axis=0).T
        weights[level] = weight_form(node[8:16])
        if level < levels - 1:
            rows = devices - (devices >> level)
            climb(held, first, devices >> (level + 1), selection_ref, rows, transfer, nodes, rows)
            held, first = nodes, rows

    def turn(at, _):
        for part in range(LEAVES_TURN):
            columns = pl.ds(pl.multiple_of((at * LEAVES_TURN + part) * tile, tile), tile)
            target = target_form(own_ref[0:8, columns])
            target = jnp.concatenate([target, jnp.zeros((LANES - 48, tile), BF16)], axis=0)
            total = jnp.zeros((16, tile), F32)
            for level in range(levels):
                total += kernel_term(sources[level], target, weights[level], rank)
            out_ref[:, columns] = (fold(total) + near_ref[:, columns]) * scale
        return 0

    lax.fori_loop(0, own_ref.shape[1] // (tile * LEAVES_TURN), turn, 0)


def far_term(scale, tile, own, near, gathered, selection, transfer):
    devices, _, rank = gathered.shape
    levels = devices.bit_length() - 1
    return pl.pallas_call(
        functools.partial(far_kernel, scale, tile),
        out_shape=jax.ShapeDtypeStruct((8, own.shape[1]), F32),
        in_specs=[VMEM_SPEC] * 5,
        out_specs=VMEM_SPEC,
        scratch_shapes=[
            pltpu.VMEM((devices - 2, 16, rank), F32),
            pltpu.VMEM((levels, rank, LANES), BF16),
            pltpu.VMEM((levels, 16, rank), BF16),
        ],
        compiler_params=pltpu.CompilerParams(vmem_limit_bytes=32 * 2**20),
        name="far_term",
    )(own, near, gathered, selection, transfer)


def body(coords, right_sides, projection, skel_index, selection, transfer, near_leaf, near_count):
    devices = lax.axis_size("leaf")
    leaves, slots = near_leaf.shape
    leaf = coords.shape[1] // leaves
    scale = 1.0 / (slots * leaf) ** 0.5
    extended, skel_index = extend(coords, right_sides, skel_index)
    chip = swap(extended, "leaf", 0)
    other = swap(extended, "leaf", 1)
    node, own_part = first_step(devices, leaf, extended, projection, skel_index)
    gathered = lax.all_to_all(node, "leaf", 0, 0, tiled=True)
    near = near_term(near_leaf, near_count, own_part, chip, extended, other)
    return far_term(scale, leaf, extended, near, gathered, selection, transfer)


def solution(mesh):
    return jax.shard_map(
        body,
        mesh=mesh,
        in_specs=(
            P(None, "leaf"),
            P(None, "leaf"),
            P("leaf", None),
            P("leaf", None),
            P(),
            P(),
            P("leaf", None),
            P("leaf"),
        ),
        out_specs=P(None, "leaf"),
        check_vma=False,
    )
```

```python
import functools
import math

import jax
import jax.numpy as jnp
from jax import lax
from jax.experimental import pallas as pl
from jax.experimental.pallas import tpu as pltpu
from jax.sharding import PartitionSpec as P

F32 = jnp.float32
BF16 = jnp.bfloat16
LANES = 128
SHIFT = 2.0
LEAVES_TURN = 8
LEAVES_SELF = 16
ROOT = math.sqrt(math.log2(math.e))
SMEM_SPEC = pl.BlockSpec(memory_space=pltpu.SMEM)
HBM_SPEC = pl.BlockSpec(memory_space=pltpu.HBM)
VMEM_SPEC = pl.BlockSpec(memory_space=pltpu.VMEM)


def swap(value, axis, first):
    count = lax.axis_size(axis)
    pairs = []
    for left in range(first, count - 1, 2):
        pairs += [(left, left + 1), (left + 1, left)]
    return lax.ppermute(value, axis, pairs)


def two_pieces(value):
    high = value.astype(BF16).astype(F32)
    return high, value - high


def three_pieces(value):
    high, rest = two_pieces(value)
    middle, low = two_pieces(rest)
    return high, middle, low


def source_form(extended):
    high, middle, low = three_pieces(extended)
    return jnp.concatenate([high, high, high, middle, middle, low], axis=0).astype(BF16)


def target_form(extended):
    row = lax.broadcasted_iota(jnp.int32, extended.shape, 0)
    below = pltpu.roll(extended, 1, 0)
    swapped = jnp.where(row == 6, 1.0, jnp.where(row == 7, below, extended))
    high, middle, low = three_pieces(swapped)
    return jnp.concatenate([high, middle, low, high, middle, high], axis=0).astype(BF16)


def weight_form(values):
    high, low = two_pieces(values)
    return jnp.concatenate([high, low], axis=0).astype(BF16)


def pick_columns(pieces, index):
    index = jnp.broadcast_to(index, (8, LANES))
    low = index & (LANES - 1)
    high = index >> 7
    result = jnp.take_along_axis(pieces[0], low, axis=1)
    for at in range(1, len(pieces)):
        result = jnp.where(high == at, jnp.take_along_axis(pieces[at], low, axis=1), result)
    return result


def split_block(exponent):
    kernel = jnp.exp2(jnp.minimum(exponent, 0.0))
    high = kernel.astype(BF16)
    return high, (kernel - high.astype(F32)).astype(BF16)


def kernel_term(source, target, weight, rows):
    highs, lows = [], []
    for first in range(0, source.shape[0], rows):
        high, low = split_block(jnp.dot(source[first:first + rows], target, preferred_element_type=F32))
        highs.append(high)
        lows.append(low)
    high = jnp.concatenate(highs, axis=0) if len(highs) > 1 else highs[0]
    low = jnp.concatenate(lows, axis=0) if len(lows) > 1 else lows[0]
    both = jnp.dot(weight, high, preferred_element_type=F32)
    return both + jnp.dot(weight, low, preferred_element_type=F32)


def fold(pieces):
    return pieces[:8] + pieces[8:]


def extend_kernel(coords_ref, right_ref, index_hbm, out_ref, index_ref, held, sems):
    rows, points = held.shape
    copies = [
        pltpu.make_async_copy(coords_ref, held, sems.at[0]),
        pltpu.make_async_copy(right_ref, out_ref.at[pl.ds(8, 8)], sems.at[1]),
        pltpu.make_async_copy(index_hbm, index_ref, sems.at[2]),
    ]
    for copy in copies:
        copy.start()
    copies[0].wait()
    centred = (held[...] - SHIFT) * ROOT
    out_ref[0:rows, :] = centred
    out_ref[rows:rows + 1, :] = -0.5 * jnp.sum(centred * centred, axis=0, keepdims=True)
    out_ref[rows + 1:rows + 2, :] = jnp.ones((1, points), F32)
    copies[1].wait()
    copies[2].wait()


def extend(coords, right_sides, skel_index):
    rows, points = coords.shape
    return pl.pallas_call(
        extend_kernel,
        out_shape=(pltpu.VMEM((16, points), F32), pltpu.VMEM(skel_index.shape, jnp.int32)),
        in_specs=[HBM_SPEC] * 3,
        out_specs=(VMEM_SPEC, VMEM_SPEC),
        scratch_shapes=[pltpu.VMEM((rows, points), F32), pltpu.SemaphoreType.DMA((3,))],
        compiler_params=pltpu.CompilerParams(vmem_limit_bytes=58 * 2**20),
        name="extend",
    )(coords, right_sides, skel_index)


def first_kernel(leaf, x_ref, proj_ref, index_ref, node_ref, self_ref, held, sources, weights, targets, sems):
    chunks = held.shape[0]
    chunk, rank = held.shape[1:]
    points = x_ref.shape[1]
    copies = [
        pltpu.make_async_copy(proj_ref.at[pl.ds(at * chunk, chunk)], held.at[at], sems.at[at]) for at in range(chunks)
    ]
    for copy in copies:
        copy.start()
    for half in range(rank // LANES):
        lanes = slice(half * LANES, (half + 1) * LANES)
        pieces = [x_ref[0:8, at * LANES:(at + 1) * LANES] for at in range(points // LANES)]
        columns = pick_columns(pieces, index_ref[:, lanes])
        for copy in range(node_ref.shape[0]):
            node_ref[copy, 0:8, lanes] = columns
    wide = 4 * leaf

    def prepare(at, _):
        columns = pl.ds(pl.multiple_of(at * wide, wide), wide)
        sources[:, columns] = source_form(x_ref[0:8, columns])
        weights[:, columns] = weight_form(x_ref[8:16, columns])
        targets[:, columns] = target_form(x_ref[0:8, columns])
        return 0

    def turn(at, _):
        for part in range(LEAVES_SELF):
            columns = pl.ds(pl.multiple_of((at * LEAVES_SELF + part) * leaf, leaf), leaf)
            self_ref[:, columns] = fold(kernel_term(sources[:, columns].T, targets[:, columns], weights[:, columns], 128))
        return 0

    lax.fori_loop(0, points // wide, prepare, 0)
    lax.fori_loop(0, points // (leaf * LEAVES_SELF), turn, 0)
    total = jnp.zeros((8, rank), F32)
    for at in range(chunks):
        x_high, x_low = two_pieces(x_ref[8:16, at * chunk:(at + 1) * chunk])
        left = jnp.concatenate([x_high, x_low], axis=0).astype(BF16)
        copies[at].wait()
        p_high, p_low = two_pieces(held[at])
        both = jnp.dot(left, p_high.astype(BF16), preferred_element_type=F32)
        part = jnp.dot(left, p_low.astype(BF16), preferred_element_type=F32)
        total += both[:8] + both[8:] + part[:8]
    for copy in range(node_ref.shape[0]):
        node_ref[copy, 8:16, :] = total


def first_step(copies, leaf, extended, projection, skel_index):
    points, rank = projection.shape
    chunks = 8
    return pl.pallas_call(
        functools.partial(first_kernel, leaf),
        out_shape=(
            jax.ShapeDtypeStruct((copies, 16, rank), F32),
            jax.ShapeDtypeStruct((8, points), F32),
        ),
        in_specs=[VMEM_SPEC, HBM_SPEC, VMEM_SPEC],
        out_specs=(VMEM_SPEC, VMEM_SPEC),
        scratch_shapes=[
            pltpu.VMEM((chunks, points // chunks, rank), F32),
            pltpu.VMEM((48, points), BF16),
            pltpu.VMEM((16, points), BF16),
            pltpu.VMEM((48, points), BF16),
            pltpu.SemaphoreType.DMA((chunks,)),
        ],
        compiler_params=pltpu.CompilerParams(vmem_limit_bytes=50 * 2**20),
        name="first_step",
    )(extended, projection, skel_index)


def climb(source, first, count, selection, rows, transfer, target, offset):
    rank = transfer[0].shape[1]
    t_high, t_low = transfer
    joined = jnp.concatenate(
        [
            jnp.concatenate([source[first + 2 * m + side, 8:16, :] for m in range(count)], axis=0)
            for side in range(2)
        ],
        axis=1,
    )
    high, low = two_pieces(joined)
    left = jnp.concatenate([high, low], axis=0).astype(BF16)
    both = jnp.dot(left, t_high, preferred_element_type=F32)
    part = jnp.dot(left, t_low, preferred_element_type=F32)
    moved = both[:8 * count] + both[8 * count:] + part[:8 * count]
    for m in range(count):
        target[offset + m, 8:16, :] = moved[m * 8:(m + 1) * 8, :]
        pieces = [
            source[first + 2 * m + side, 0:8, at * LANES:(at + 1) * LANES]
            for side in range(2)
            for at in range(rank // LANES)
        ]
        picked = selection[pl.ds(rows + m, 1), :]
        for half in range(rank // LANES):
            lanes = slice(half * LANES, (half + 1) * LANES)
            target[offset + m, 0:8, lanes] = pick_columns(pieces, picked[:, lanes])


def split_transfer(transfer_ref):
    t_high, t_low = two_pieces(transfer_ref[...])
    return t_high.astype(BF16), t_low.astype(BF16)


def near_kernel(near_ref, count_ref, self_ref, chip_ref, own_ref, other_ref, out_ref, sources, weights, targets):
    leaves, slots = near_ref.shape
    points = own_ref.shape[1]
    leaf = points // leaves
    own_index = lax.axis_index("leaf")
    even = own_index % 2 == 0
    first_leaf = own_index * leaves
    wide = 4 * leaf

    def prepare(at, _):
        columns = pl.ds(pl.multiple_of(at * wide, wide), wide)
        for part, ref in enumerate((chip_ref, own_ref, other_ref)):
            window = pl.ds(pl.multiple_of(part * points + at * wide, wide), wide)
            sources[:, window] = source_form(ref[0:8, columns])
            weights[:, window] = weight_form(ref[8:16, columns])
        targets[:, columns] = target_form(own_ref[0:8, columns])
        return 0

    lax.fori_loop(0, points // wide, prepare, 0)

    def window_place(offset):
        below, above = offset < 0, offset >= leaves
        left = jnp.where(even, 2, 0)
        part = jnp.where(below, left, jnp.where(above, 2 - left, 1))
        local = jnp.where(below, offset + leaves, jnp.where(above, offset - leaves, offset))
        return part * leaves + jnp.clip(local, 0, leaves - 1)

    def one_leaf(at, live_slots):
        columns = pl.ds(pl.multiple_of(at * leaf, leaf), leaf)
        target = targets[:, columns]
        total = jnp.zeros((16, leaf), F32)
        for slot in range(1, live_slots):
            place = window_place(near_ref[at, slot] - first_leaf)
            window = pl.ds(pl.multiple_of(place * leaf, leaf), leaf)
            weight = weights[:, window]
            weight = jnp.where(slot < count_ref[at], weight, jnp.zeros_like(weight))
            total += kernel_term(sources[:, window].T, target, weight, 128)
        out_ref[:, columns] = self_ref[:, columns] + fold(total)

    def turn(at, _):
        most = count_ref[LEAVES_TURN * at]
        for leaf_at in range(1, LEAVES_TURN):
            most = jnp.maximum(most, count_ref[LEAVES_TURN * at + leaf_at])
        heavy = most > slots // 2

        @pl.when(heavy)
        def _():
            for leaf_at in range(LEAVES_TURN):
                one_leaf(LEAVES_TURN * at + leaf_at, slots)

        @pl.when(jnp.logical_not(heavy))
        def _():
            for leaf_at in range(LEAVES_TURN):
                one_leaf(LEAVES_TURN * at + leaf_at, slots // 2)

        return 0

    lax.fori_loop(0, leaves // LEAVES_TURN, turn, 0)


def near_term(near_leaf, near_count, own_part, chip, own, other):
    leaves, slots = near_leaf.shape
    points = own.shape[1]
    entries = leaves * slots * (points // leaves) ** 2
    return pl.pallas_call(
        near_kernel,
        out_shape=jax.ShapeDtypeStruct((8, points), F32),
        in_specs=[SMEM_SPEC] * 2 + [VMEM_SPEC] * 4,
        out_specs=VMEM_SPEC,
        scratch_shapes=[
            pltpu.VMEM((48, 3 * points), BF16),
            pltpu.VMEM((16, 3 * points), BF16),
            pltpu.VMEM((48, points), BF16),
        ],
        cost_estimate=pl.CostEstimate(flops=1000 * entries, bytes_accessed=4 * 64 * points, transcendentals=entries),
        compiler_params=pltpu.CompilerParams(vmem_limit_bytes=32 * 2**20),
        name="near_term",
    )(near_leaf, near_count, own_part, chip, own, other)


def far_kernel(scale, tile, own_ref, near_ref, gathered_ref, selection_ref, transfer_ref, out_ref, nodes, sources, weights):
    devices = gathered_ref.shape[0]
    levels = devices.bit_length() - 1
    own_index = lax.axis_index("leaf")
    transfer = split_transfer(transfer_ref)
    rank = transfer_ref.shape[1]
    held, first = gathered_ref, 0
    for level in range(levels):
        node = held[first + ((own_index >> level) ^ 1)]
        form = source_form(node[0:8])
        sources[level] = jnp.concatenate([form, jnp.zeros((LANES - 48, rank), BF16)], axis=0).T
        weights[level] = weight_form(node[8:16])
        if level < levels - 1:
            rows = devices - (devices >> level)
            climb(held, first, devices >> (level + 1), selection_ref, rows, transfer, nodes, rows)
            held, first = nodes, rows

    def turn(at, _):
        for part in range(LEAVES_TURN):
            columns = pl.ds(pl.multiple_of((at * LEAVES_TURN + part) * tile, tile), tile)
            target = target_form(own_ref[0:8, columns])
            target = jnp.concatenate([target, jnp.zeros((LANES - 48, tile), BF16)], axis=0)
            total = jnp.zeros((16, tile), F32)
            for level in range(levels):
                total += kernel_term(sources[level], target, weights[level], rank)
            out_ref[:, columns] = (fold(total) + near_ref[:, columns]) * scale
        return 0

    lax.fori_loop(0, own_ref.shape[1] // (tile * LEAVES_TURN), turn, 0)


def far_term(scale, tile, own, near, gathered, selection, transfer):
    devices, _, rank = gathered.shape
    levels = devices.bit_length() - 1
    return pl.pallas_call(
        functools.partial(far_kernel, scale, tile),
        out_shape=jax.ShapeDtypeStruct((8, own.shape[1]), F32),
        in_specs=[VMEM_SPEC] * 5,
        out_specs=VMEM_SPEC,
        scratch_shapes=[
            pltpu.VMEM((devices - 2, 16, rank), F32),
            pltpu.VMEM((levels, rank, LANES), BF16),
            pltpu.VMEM((levels, 16, rank), BF16),
        ],
        compiler_params=pltpu.CompilerParams(vmem_limit_bytes=32 * 2**20),
        name="far_term",
    )(own, near, gathered, selection, transfer)


def body(coords, right_sides, projection, skel_index, selection, transfer, near_leaf, near_count):
    devices = lax.axis_size("leaf")
    leaves, slots = near_leaf.shape
    leaf = coords.shape[1] // leaves
    scale = 1.0 / (slots * leaf) ** 0.5
    extended, skel_index = extend(coords, right_sides, skel_index)
    chip = swap(extended, "leaf", 0)
    other = swap(extended, "leaf", 1)
    node, own_part = first_step(devices, leaf, extended, projection, skel_index)
    gathered = lax.all_to_all(node, "leaf", 0, 0, tiled=True)
    near = near_term(near_leaf, near_count, own_part, chip, extended, other)
    return far_term(scale, leaf, extended, near, gathered, selection, transfer)


def solution(mesh):
    return jax.shard_map(
        body,
        mesh=mesh,
        in_specs=(
            P(None, "leaf"),
            P(None, "leaf"),
            P("leaf", None),
            P("leaf", None),
            P(),
            P(),
            P("leaf", None),
            P("leaf"),
        ),
        out_specs=P(None, "leaf"),
        check_vma=False,
    )
```

```python
import functools
import math

import jax
import jax.numpy as jnp
from jax import lax
from jax.experimental import pallas as pl
from jax.experimental.pallas import tpu as pltpu
from jax.sharding import PartitionSpec as P

F32 = jnp.float32
BF16 = jnp.bfloat16
LANES = 128
ROWS = 32
SHIFT = 2.0
LEAVES_TURN = 16
LEAVES_SELF = 16
ROOT = math.sqrt(math.log2(math.e))
SMEM_SPEC = pl.BlockSpec(memory_space=pltpu.SMEM)
HBM_SPEC = pl.BlockSpec(memory_space=pltpu.HBM)
VMEM_SPEC = pl.BlockSpec(memory_space=pltpu.VMEM)


def swap(value, axis, first):
    count = lax.axis_size(axis)
    pairs = []
    for left in range(first, count - 1, 2):
        pairs += [(left, left + 1), (left + 1, left)]
    return lax.ppermute(value, axis, pairs)


def two_pieces(value):
    high = value.astype(BF16).astype(F32)
    return high, value - high


def extended_pieces(extended):
    high, rest = two_pieces(extended)
    middle, low = two_pieces(rest)
    row = lax.broadcasted_iota(jnp.int32, extended.shape, 0)
    return high, middle, jnp.where(row < 6, middle, low), row


def source_form(extended):
    high, middle, last, row = extended_pieces(extended)
    last = jnp.where(row == 7, 1.0, last)
    return jnp.concatenate([high, high, middle, last], axis=0).astype(BF16)


def target_form(extended):
    row = lax.broadcasted_iota(jnp.int32, extended.shape, 0)
    below = pltpu.roll(extended, 1, 0)
    swapped = jnp.where(row == 6, 1.0, jnp.where(row == 7, below, extended))
    high, middle, last, _ = extended_pieces(swapped)
    last = jnp.where(row == 6, 1.0, last)
    return jnp.concatenate([high, middle, high, last], axis=0).astype(BF16)


def weight_form(values):
    high, low = two_pieces(values)
    return jnp.concatenate([high, low], axis=0).astype(BF16)


def pick_columns(pieces, index):
    index = jnp.broadcast_to(index, (8, LANES))
    low = index & (LANES - 1)
    high = index >> 7
    result = jnp.take_along_axis(pieces[0], low, axis=1)
    for at in range(1, len(pieces)):
        result = jnp.where(high == at, jnp.take_along_axis(pieces[at], low, axis=1), result)
    return result


def split_block(exponent):
    kernel = jnp.exp2(jnp.minimum(exponent, 0.0))
    high = kernel.astype(BF16)
    return high, (kernel - high.astype(F32)).astype(BF16)


def repeat_blocks(weight):
    pieces = []
    for first in range(0, weight.shape[1], LANES):
        pieces += [weight[:, first:first + LANES]] * 2
    return jnp.concatenate(pieces, axis=1)


def kernel_pieces(source, target):
    pieces = []
    for first in range(0, source.shape[0], LANES):
        pieces += split_block(jnp.dot(source[first:first + LANES], target, preferred_element_type=F32))
    return pieces


def weigh(weights, pieces):
    weights = jnp.concatenate(weights, axis=1) if len(weights) > 1 else weights[0]
    return fold(jnp.dot(weights, jnp.concatenate(pieces, axis=0), preferred_element_type=F32))


def fold(pieces):
    return pieces[:8] + pieces[8:]


def extend_kernel(coords_ref, right_ref, index_hbm, out_ref, index_ref, held, sems):
    rows, points = held.shape
    copies = [
        pltpu.make_async_copy(coords_ref, held, sems.at[0]),
        pltpu.make_async_copy(right_ref, out_ref.at[pl.ds(8, 8)], sems.at[1]),
        pltpu.make_async_copy(index_hbm, index_ref, sems.at[2]),
    ]
    for copy in copies:
        copy.start()
    copies[0].wait()
    centred = (held[...] - SHIFT) * ROOT
    out_ref[0:rows, :] = centred
    out_ref[rows:rows + 1, :] = -0.5 * jnp.sum(centred * centred, axis=0, keepdims=True)
    out_ref[rows + 1:rows + 2, :] = jnp.ones((1, points), F32)
    copies[1].wait()
    copies[2].wait()


def extend(coords, right_sides, skel_index):
    rows, points = coords.shape
    return pl.pallas_call(
        extend_kernel,
        out_shape=(pltpu.VMEM((16, points), F32), pltpu.VMEM(skel_index.shape, jnp.int32)),
        in_specs=[HBM_SPEC] * 3,
        out_specs=(VMEM_SPEC, VMEM_SPEC),
        scratch_shapes=[pltpu.VMEM((rows, points), F32), pltpu.SemaphoreType.DMA((3,))],
        compiler_params=pltpu.CompilerParams(vmem_limit_bytes=58 * 2**20),
        name="extend",
    )(coords, right_sides, skel_index)


def first_kernel(leaf, x_ref, proj_ref, index_ref, node_ref, self_ref, held, sources, weights, targets, sems):
    chunks = held.shape[0]
    chunk, rank = held.shape[1:]
    points = x_ref.shape[1]
    copies = [
        pltpu.make_async_copy(proj_ref.at[pl.ds(at * chunk, chunk)], held.at[at], sems.at[at]) for at in range(chunks)
    ]
    for copy in copies:
        copy.start()
    for half in range(rank // LANES):
        lanes = slice(half * LANES, (half + 1) * LANES)
        pieces = [x_ref[0:8, at * LANES:(at + 1) * LANES] for at in range(points // LANES)]
        columns = pick_columns(pieces, index_ref[:, lanes])
        for copy in range(node_ref.shape[0]):
            node_ref[copy, 0:8, lanes] = columns
    wide = 4 * leaf

    def prepare(at, _):
        columns = pl.ds(pl.multiple_of(at * wide, wide), wide)
        sources[:, columns] = source_form(x_ref[0:8, columns])
        twice = pl.ds(pl.multiple_of(at * 2 * wide, wide), 2 * wide)
        weights[:, twice] = repeat_blocks(weight_form(x_ref[8:16, columns]))
        targets[:, columns] = target_form(x_ref[0:8, columns])
        return 0

    def turn(at, _):
        for part in range(LEAVES_SELF):
            columns = pl.ds(pl.multiple_of((at * LEAVES_SELF + part) * leaf, leaf), leaf)
            twice = pl.ds(pl.multiple_of((at * LEAVES_SELF + part) * 2 * leaf, leaf), 2 * leaf)
            pieces = kernel_pieces(sources[:, columns].T, targets[:, columns])
            self_ref[:, columns] = weigh([weights[:, twice]], pieces)
        return 0

    lax.fori_loop(0, points // wide, prepare, 0)
    lax.fori_loop(0, points // (leaf * LEAVES_SELF), turn, 0)
    total = jnp.zeros((8, rank), F32)
    for at in range(chunks):
        x_high, x_low = two_pieces(x_ref[8:16, at * chunk:(at + 1) * chunk])
        left = jnp.concatenate([x_high, x_low], axis=0).astype(BF16)
        copies[at].wait()
        p_high, p_low = two_pieces(held[at])
        both = jnp.dot(left, p_high.astype(BF16), preferred_element_type=F32)
        part = jnp.dot(left, p_low.astype(BF16), preferred_element_type=F32)
        total += both[:8] + both[8:] + part[:8]
    for copy in range(node_ref.shape[0]):
        node_ref[copy, 8:16, :] = total


def first_step(copies, leaf, extended, projection, skel_index):
    points, rank = projection.shape
    chunks = 8
    return pl.pallas_call(
        functools.partial(first_kernel, leaf),
        out_shape=(
            jax.ShapeDtypeStruct((copies, 16, rank), F32),
            jax.ShapeDtypeStruct((8, points), F32),
        ),
        in_specs=[VMEM_SPEC, HBM_SPEC, VMEM_SPEC],
        out_specs=(VMEM_SPEC, VMEM_SPEC),
        scratch_shapes=[
            pltpu.VMEM((chunks, points // chunks, rank), F32),
            pltpu.VMEM((ROWS, points), BF16),
            pltpu.VMEM((16, 2 * points), BF16),
            pltpu.VMEM((ROWS, points), BF16),
            pltpu.SemaphoreType.DMA((chunks,)),
        ],
        compiler_params=pltpu.CompilerParams(vmem_limit_bytes=50 * 2**20),
        name="first_step",
    )(extended, projection, skel_index)


def climb(source, first, count, selection, rows, transfer, target, offset):
    rank = transfer[0].shape[1]
    t_high, t_low = transfer
    joined = jnp.concatenate(
        [
            jnp.concatenate([source[first + 2 * m + side, 8:16, :] for m in range(count)], axis=0)
            for side in range(2)
        ],
        axis=1,
    )
    high, low = two_pieces(joined)
    left = jnp.concatenate([high, low], axis=0).astype(BF16)
    both = jnp.dot(left, t_high, preferred_element_type=F32)
    part = jnp.dot(left, t_low, preferred_element_type=F32)
    moved = both[:8 * count] + both[8 * count:] + part[:8 * count]
    for m in range(count):
        target[offset + m, 8:16, :] = moved[m * 8:(m + 1) * 8, :]
        pieces = [
            source[first + 2 * m + side, 0:8, at * LANES:(at + 1) * LANES]
            for side in range(2)
            for at in range(rank // LANES)
        ]
        picked = selection[pl.ds(rows + m, 1), :]
        for half in range(rank // LANES):
            lanes = slice(half * LANES, (half + 1) * LANES)
            target[offset + m, 0:8, lanes] = pick_columns(pieces, picked[:, lanes])


def split_transfer(transfer_ref):
    t_high, t_low = two_pieces(transfer_ref[...])
    return t_high.astype(BF16), t_low.astype(BF16)


def near_kernel(near_ref, count_ref, self_ref, chip_ref, own_ref, other_ref, out_ref, sources, weights, targets):
    leaves, slots = near_ref.shape
    points = own_ref.shape[1]
    leaf = points // leaves
    own_index = lax.axis_index("leaf")
    even = own_index % 2 == 0
    first_leaf = own_index * leaves
    wide = 4 * leaf

    def prepare(at, _):
        columns = pl.ds(pl.multiple_of(at * wide, wide), wide)
        for part, ref in enumerate((chip_ref, own_ref, other_ref)):
            window = pl.ds(pl.multiple_of(part * points + at * wide, wide), wide)
            sources[:, window] = source_form(ref[0:8, columns])
            twice = pl.ds(pl.multiple_of(2 * (part * points + at * wide), wide), 2 * wide)
            weights[:, twice] = repeat_blocks(weight_form(ref[8:16, columns]))
        targets[:, columns] = target_form(own_ref[0:8, columns])
        return 0

    lax.fori_loop(0, points // wide, prepare, 0)

    def window_place(offset):
        below, above = offset < 0, offset >= leaves
        left = jnp.where(even, 2, 0)
        part = jnp.where(below, left, jnp.where(above, 2 - left, 1))
        local = jnp.where(below, offset + leaves, jnp.where(above, offset - leaves, offset))
        return part * leaves + jnp.clip(local, 0, leaves - 1)

    def one_leaf(at, live_slots):
        columns = pl.ds(pl.multiple_of(at * leaf, leaf), leaf)
        target = targets[:, columns]
        held, pieces = [], []
        for slot in range(1, live_slots):
            place = window_place(near_ref[at, slot] - first_leaf)
            window = pl.ds(pl.multiple_of(place * leaf, leaf), leaf)
            weight = weights[:, pl.ds(pl.multiple_of(place * 2 * leaf, leaf), 2 * leaf)]
            held.append(jnp.where(slot < count_ref[at], weight, jnp.zeros_like(weight)))
            pieces += kernel_pieces(sources[:, window].T, target)
        out_ref[:, columns] = self_ref[:, columns] + weigh(held, pieces)

    def turn(at, _):
        most = count_ref[LEAVES_TURN * at]
        for leaf_at in range(1, LEAVES_TURN):
            most = jnp.maximum(most, count_ref[LEAVES_TURN * at + leaf_at])
        heavy = most > slots // 2

        @pl.when(heavy)
        def _():
            for leaf_at in range(LEAVES_TURN):
                one_leaf(LEAVES_TURN * at + leaf_at, slots)

        @pl.when(jnp.logical_not(heavy))
        def _():
            for leaf_at in range(LEAVES_TURN):
                one_leaf(LEAVES_TURN * at + leaf_at, slots // 2)

        return 0

    lax.fori_loop(0, leaves // LEAVES_TURN, turn, 0)


def near_term(near_leaf, near_count, own_part, chip, own, other):
    leaves, slots = near_leaf.shape
    points = own.shape[1]
    entries = leaves * slots * (points // leaves) ** 2
    return pl.pallas_call(
        near_kernel,
        out_shape=jax.ShapeDtypeStruct((8, points), F32),
        in_specs=[SMEM_SPEC] * 2 + [VMEM_SPEC] * 4,
        out_specs=VMEM_SPEC,
        scratch_shapes=[
            pltpu.VMEM((ROWS, 3 * points), BF16),
            pltpu.VMEM((16, 6 * points), BF16),
            pltpu.VMEM((ROWS, points), BF16),
        ],
        cost_estimate=pl.CostEstimate(flops=1000 * entries, bytes_accessed=4 * 64 * points, transcendentals=entries),
        compiler_params=pltpu.CompilerParams(vmem_limit_bytes=32 * 2**20),
        name="near_term",
    )(near_leaf, near_count, own_part, chip, own, other)


def far_kernel(scale, tile, own_ref, near_ref, gathered_ref, selection_ref, transfer_ref, out_ref, nodes, sources, weights):
    devices = gathered_ref.shape[0]
    levels = devices.bit_length() - 1
    own_index = lax.axis_index("leaf")
    transfer = split_transfer(transfer_ref)
    rank = transfer_ref.shape[1]
    held, first = gathered_ref, 0
    for level in range(levels):
        node = held[first + ((own_index >> level) ^ 1)]
        form = source_form(node[0:8])
        sources[level] = jnp.concatenate([form, jnp.zeros((LANES - ROWS, rank), BF16)], axis=0).T
        weights[level] = repeat_blocks(weight_form(node[8:16]))
        if level < levels - 1:
            rows = devices - (devices >> level)
            climb(held, first, devices >> (level + 1), selection_ref, rows, transfer, nodes, rows)
            held, first = nodes, rows

    def turn(at, _):
        for part in range(LEAVES_TURN):
            columns = pl.ds(pl.multiple_of((at * LEAVES_TURN + part) * tile, tile), tile)
            target = target_form(own_ref[0:8, columns])
            target = jnp.concatenate([target, jnp.zeros((LANES - ROWS, tile), BF16)], axis=0)
            pieces = []
            for level in range(levels):
                pieces += kernel_pieces(sources[level], target)
            total = weigh([weights[level] for level in range(levels)], pieces)
            out_ref[:, columns] = (total + near_ref[:, columns]) * scale
        return 0

    lax.fori_loop(0, own_ref.shape[1] // (tile * LEAVES_TURN), turn, 0)


def far_term(scale, tile, own, near, gathered, selection, transfer):
    devices, _, rank = gathered.shape
    levels = devices.bit_length() - 1
    return pl.pallas_call(
        functools.partial(far_kernel, scale, tile),
        out_shape=jax.ShapeDtypeStruct((8, own.shape[1]), F32),
        in_specs=[VMEM_SPEC] * 5,
        out_specs=VMEM_SPEC,
        scratch_shapes=[
            pltpu.VMEM((devices - 2, 16, rank), F32),
            pltpu.VMEM((levels, rank, LANES), BF16),
            pltpu.VMEM((levels, 16, 2 * rank), BF16),
        ],
        compiler_params=pltpu.CompilerParams(vmem_limit_bytes=32 * 2**20),
        name="far_term",
    )(own, near, gathered, selection, transfer)


def body(coords, right_sides, projection, skel_index, selection, transfer, near_leaf, near_count):
    devices = lax.axis_size("leaf")
    leaves, slots = near_leaf.shape
    leaf = coords.shape[1] // leaves
    scale = 1.0 / (slots * leaf) ** 0.5
    extended, skel_index = extend(coords, right_sides, skel_index)
    chip = swap(extended, "leaf", 0)
    other = swap(extended, "leaf", 1)
    node, own_part = first_step(devices, leaf, extended, projection, skel_index)
    gathered = lax.all_to_all(node, "leaf", 0, 0, tiled=True)
    near = near_term(near_leaf, near_count, own_part, chip, extended, other)
    return far_term(scale, leaf, extended, near, gathered, selection, transfer)


def solution(mesh):
    return jax.shard_map(
        body,
        mesh=mesh,
        in_specs=(
            P(None, "leaf"),
            P(None, "leaf"),
            P("leaf", None),
            P("leaf", None),
            P(),
            P(),
            P("leaf", None),
            P("leaf"),
        ),
        out_specs=P(None, "leaf"),
        check_vma=False,
    )
```

```python
import functools
import math

import jax
import jax.numpy as jnp
from jax import lax
from jax.experimental import pallas as pl
from jax.experimental.pallas import tpu as pltpu
from jax.sharding import PartitionSpec as P

F32 = jnp.float32
BF16 = jnp.bfloat16
LANES = 128
SHIFT = 2.0
NEAR_TURN = 16
FAR_TURN = 32
LEAVES_SELF = 16
ROOT = math.sqrt(math.log2(math.e))
SMEM_SPEC = pl.BlockSpec(memory_space=pltpu.SMEM)
HBM_SPEC = pl.BlockSpec(memory_space=pltpu.HBM)
VMEM_SPEC = pl.BlockSpec(memory_space=pltpu.VMEM)


def swap(value, axis, first):
    count = lax.axis_size(axis)
    pairs = []
    for left in range(first, count - 1, 2):
        pairs += [(left, left + 1), (left + 1, left)]
    return lax.ppermute(value, axis, pairs)


def two_pieces(value):
    high = value.astype(BF16).astype(F32)
    return high, value - high


def three_pieces(value):
    high, rest = two_pieces(value)
    middle, low = two_pieces(rest)
    return high, middle, low


def source_form(extended):
    high, middle, low = three_pieces(extended)
    return jnp.concatenate([high, high, high, middle, middle, low], axis=0).astype(BF16)


def target_form(extended):
    row = lax.broadcasted_iota(jnp.int32, extended.shape, 0)
    below = pltpu.roll(extended, 1, 0)
    swapped = jnp.where(row == 6, 1.0, jnp.where(row == 7, below, extended))
    high, middle, low = three_pieces(swapped)
    return jnp.concatenate([high, middle, low, high, middle, high], axis=0).astype(BF16)


def weight_form(values):
    high, low = two_pieces(values)
    return jnp.concatenate([high, low], axis=0).astype(BF16)


def pick_columns(pieces, index):
    index = jnp.broadcast_to(index, (8, LANES))
    low = index & (LANES - 1)
    high = index >> 7
    result = jnp.take_along_axis(pieces[0], low, axis=1)
    for at in range(1, len(pieces)):
        result = jnp.where(high == at, jnp.take_along_axis(pieces[at], low, axis=1), result)
    return result


def split_block(exponent):
    kernel = jnp.exp2(jnp.minimum(exponent, 0.0))
    high = kernel.astype(BF16)
    return high, (kernel - high.astype(F32)).astype(BF16)


def repeat_blocks(weight):
    pieces = []
    for first in range(0, weight.shape[1], LANES):
        pieces += [weight[:, first:first + LANES]] * 2
    return jnp.concatenate(pieces, axis=1)


def kernel_term(source, target, weight):
    total = None
    for first in range(0, source.shape[0], LANES):
        high, low = split_block(jnp.dot(source[first:first + LANES], target, preferred_element_type=F32))
        both = jnp.concatenate([high, low], axis=0)
        term = jnp.dot(weight[:, 2 * first:2 * (first + LANES)], both, preferred_element_type=F32)
        total = term if total is None else total + term
    return total


def kernel_pieces(source, target):
    pieces = []
    for first in range(0, source.shape[0], LANES):
        pieces += split_block(jnp.dot(source[first:first + LANES], target, preferred_element_type=F32))
    return pieces


def weigh(weights, pieces):
    weights = jnp.concatenate(weights, axis=1)
    return fold(jnp.dot(weights, jnp.concatenate(pieces, axis=0), preferred_element_type=F32))


def fold(pieces):
    return pieces[:8] + pieces[8:]


def extend_kernel(coords_ref, right_ref, index_hbm, out_ref, index_ref, held, sems):
    rows, points = held.shape
    copies = [
        pltpu.make_async_copy(coords_ref, held, sems.at[0]),
        pltpu.make_async_copy(right_ref, out_ref.at[pl.ds(8, 8)], sems.at[1]),
        pltpu.make_async_copy(index_hbm, index_ref, sems.at[2]),
    ]
    for copy in copies:
        copy.start()
    copies[0].wait()
    centred = (held[...] - SHIFT) * ROOT
    out_ref[0:rows, :] = centred
    out_ref[rows:rows + 1, :] = -0.5 * jnp.sum(centred * centred, axis=0, keepdims=True)
    out_ref[rows + 1:rows + 2, :] = jnp.ones((1, points), F32)
    copies[1].wait()
    copies[2].wait()


def extend(coords, right_sides, skel_index):
    rows, points = coords.shape
    return pl.pallas_call(
        extend_kernel,
        out_shape=(pltpu.VMEM((16, points), F32), pltpu.VMEM(skel_index.shape, jnp.int32)),
        in_specs=[HBM_SPEC] * 3,
        out_specs=(VMEM_SPEC, VMEM_SPEC),
        scratch_shapes=[pltpu.VMEM((rows, points), F32), pltpu.SemaphoreType.DMA((3,))],
        compiler_params=pltpu.CompilerParams(vmem_limit_bytes=58 * 2**20),
        name="extend",
    )(coords, right_sides, skel_index)


def first_kernel(leaf, x_ref, proj_ref, index_ref, node_ref, self_ref, held, sources, weights, targets, sems):
    chunks = held.shape[0]
    chunk, rank = held.shape[1:]
    points = x_ref.shape[1]
    copies = [
        pltpu.make_async_copy(proj_ref.at[pl.ds(at * chunk, chunk)], held.at[at], sems.at[at]) for at in range(chunks)
    ]
    for copy in copies:
        copy.start()
    for half in range(rank // LANES):
        lanes = slice(half * LANES, (half + 1) * LANES)
        pieces = [x_ref[0:8, at * LANES:(at + 1) * LANES] for at in range(points // LANES)]
        columns = pick_columns(pieces, index_ref[:, lanes])
        for copy in range(node_ref.shape[0]):
            node_ref[copy, 0:8, lanes] = columns
    wide = 8 * leaf

    def prepare(at, _):
        columns = pl.ds(pl.multiple_of(at * wide, wide), wide)
        sources[:, columns] = source_form(x_ref[0:8, columns])
        twice = pl.ds(pl.multiple_of(at * 2 * wide, wide), 2 * wide)
        weights[:, twice] = repeat_blocks(weight_form(x_ref[8:16, columns]))
        targets[:, columns] = target_form(x_ref[0:8, columns])
        return 0

    def turn(at, _):
        for part in range(LEAVES_SELF):
            columns = pl.ds(pl.multiple_of((at * LEAVES_SELF + part) * leaf, leaf), leaf)
            twice = pl.ds(pl.multiple_of((at * LEAVES_SELF + part) * 2 * leaf, leaf), 2 * leaf)
            self_ref[:, columns] = fold(kernel_term(sources[:, columns].T, targets[:, columns], weights[:, twice]))
        return 0

    lax.fori_loop(0, points // wide, prepare, 0)
    lax.fori_loop(0, points // (leaf * LEAVES_SELF), turn, 0)
    total = jnp.zeros((8, rank), F32)
    for at in range(chunks):
        x_high, x_low = two_pieces(x_ref[8:16, at * chunk:(at + 1) * chunk])
        left = jnp.concatenate([x_high, x_low], axis=0).astype(BF16)
        copies[at].wait()
        p_high, p_low = two_pieces(held[at])
        both = jnp.dot(left, p_high.astype(BF16), preferred_element_type=F32)
        part = jnp.dot(left, p_low.astype(BF16), preferred_element_type=F32)
        total += both[:8] + both[8:] + part[:8]
    for copy in range(node_ref.shape[0]):
        node_ref[copy, 8:16, :] = total


def first_step(copies, leaf, extended, projection, skel_index):
    points, rank = projection.shape
    chunks = 8
    return pl.pallas_call(
        functools.partial(first_kernel, leaf),
        out_shape=(
            jax.ShapeDtypeStruct((copies, 16, rank), F32),
            jax.ShapeDtypeStruct((8, points), F32),
        ),
        in_specs=[VMEM_SPEC, HBM_SPEC, VMEM_SPEC],
        out_specs=(VMEM_SPEC, VMEM_SPEC),
        scratch_shapes=[
            pltpu.VMEM((chunks, points // chunks, rank), F32),
            pltpu.VMEM((48, points), BF16),
            pltpu.VMEM((16, 2 * points), BF16),
            pltpu.VMEM((48, points), BF16),
            pltpu.SemaphoreType.DMA((chunks,)),
        ],
        compiler_params=pltpu.CompilerParams(vmem_limit_bytes=50 * 2**20),
        name="first_step",
    )(extended, projection, skel_index)


def climb(source, first, count, selection, rows, transfer, target, offset):
    rank = transfer[0].shape[1]
    t_high, t_low = transfer
    joined = jnp.concatenate(
        [
            jnp.concatenate([source[first + 2 * m + side, 8:16, :] for m in range(count)], axis=0)
            for side in range(2)
        ],
        axis=1,
    )
    high, low = two_pieces(joined)
    left = jnp.concatenate([high, low], axis=0).astype(BF16)
    both = jnp.dot(left, t_high, preferred_element_type=F32)
    part = jnp.dot(left, t_low, preferred_element_type=F32)
    moved = both[:8 * count] + both[8 * count:] + part[:8 * count]
    for m in range(count):
        target[offset + m, 8:16, :] = moved[m * 8:(m + 1) * 8, :]
        pieces = [
            source[first + 2 * m + side, 0:8, at * LANES:(at + 1) * LANES]
            for side in range(2)
            for at in range(rank // LANES)
        ]
        picked = selection[pl.ds(rows + m, 1), :]
        for half in range(rank // LANES):
            lanes = slice(half * LANES, (half + 1) * LANES)
            target[offset + m, 0:8, lanes] = pick_columns(pieces, picked[:, lanes])


def split_transfer(transfer_ref):
    t_high, t_low = two_pieces(transfer_ref[...])
    return t_high.astype(BF16), t_low.astype(BF16)


def near_kernel(near_ref, count_ref, self_ref, chip_ref, own_ref, other_ref, out_ref, sources, weights, targets):
    leaves, slots = near_ref.shape
    points = own_ref.shape[1]
    leaf = points // leaves
    own_index = lax.axis_index("leaf")
    even = own_index % 2 == 0
    first_leaf = own_index * leaves
    wide = 8 * leaf

    def prepare(at, _):
        columns = pl.ds(pl.multiple_of(at * wide, wide), wide)
        for part, ref in enumerate((chip_ref, own_ref, other_ref)):
            window = pl.ds(pl.multiple_of(part * points + at * wide, wide), wide)
            sources[:, window] = source_form(ref[0:8, columns])
            twice = pl.ds(pl.multiple_of(2 * (part * points + at * wide), wide), 2 * wide)
            weights[:, twice] = repeat_blocks(weight_form(ref[8:16, columns]))
        targets[:, columns] = target_form(own_ref[0:8, columns])
        return 0

    lax.fori_loop(0, points // wide, prepare, 0)

    def window_place(offset):
        below, above = offset < 0, offset >= leaves
        left = jnp.where(even, 2, 0)
        part = jnp.where(below, left, jnp.where(above, 2 - left, 1))
        local = jnp.where(below, offset + leaves, jnp.where(above, offset - leaves, offset))
        return part * leaves + jnp.clip(local, 0, leaves - 1)

    def one_leaf(at, live_slots):
        columns = pl.ds(pl.multiple_of(at * leaf, leaf), leaf)
        target = targets[:, columns]
        held, pieces = [], []
        for slot in range(1, live_slots):
            place = window_place(near_ref[at, slot] - first_leaf)
            window = pl.ds(pl.multiple_of(place * leaf, leaf), leaf)
            weight = weights[:, pl.ds(pl.multiple_of(place * 2 * leaf, leaf), 2 * leaf)]
            held.append(jnp.where(slot < count_ref[at], weight, jnp.zeros_like(weight)))
            pieces += kernel_pieces(sources[:, window].T, target)
        out_ref[:, columns] = self_ref[:, columns] + weigh(held, pieces)

    def turn(at, _):
        most = count_ref[NEAR_TURN * at]
        for leaf_at in range(1, NEAR_TURN):
            most = jnp.maximum(most, count_ref[NEAR_TURN * at + leaf_at])
        heavy = most > slots // 2

        @pl.when(heavy)
        def _():
            for leaf_at in range(NEAR_TURN):
                one_leaf(NEAR_TURN * at + leaf_at, slots)

        @pl.when(jnp.logical_not(heavy))
        def _():
            for leaf_at in range(NEAR_TURN):
                one_leaf(NEAR_TURN * at + leaf_at, slots // 2)

        return 0

    lax.fori_loop(0, leaves // NEAR_TURN, turn, 0)


def near_term(near_leaf, near_count, own_part, chip, own, other):
    leaves, slots = near_leaf.shape
    points = own.shape[1]
    entries = leaves * slots * (points // leaves) ** 2
    return pl.pallas_call(
        near_kernel,
        out_shape=jax.ShapeDtypeStruct((8, points), F32),
        in_specs=[SMEM_SPEC] * 2 + [VMEM_SPEC] * 4,
        out_specs=VMEM_SPEC,
        scratch_shapes=[
            pltpu.VMEM((48, 3 * points), BF16),
            pltpu.VMEM((16, 6 * points), BF16),
            pltpu.VMEM((48, points), BF16),
        ],
        cost_estimate=pl.CostEstimate(flops=1000 * entries, bytes_accessed=4 * 64 * points, transcendentals=entries),
        compiler_params=pltpu.CompilerParams(vmem_limit_bytes=32 * 2**20),
        name="near_term",
    )(near_leaf, near_count, own_part, chip, own, other)


def far_kernel(scale, tile, own_ref, near_ref, gathered_ref, selection_ref, transfer_ref, out_ref, nodes, sources, weights):
    devices = gathered_ref.shape[0]
    levels = devices.bit_length() - 1
    own_index = lax.axis_index("leaf")
    transfer = split_transfer(transfer_ref)
    rank = transfer_ref.shape[1]
    held, first = gathered_ref, 0
    for level in range(levels):
        node = held[first + ((own_index >> level) ^ 1)]
        form = source_form(node[0:8])
        sources[level] = jnp.concatenate([form, jnp.zeros((LANES - 48, rank), BF16)], axis=0).T
        weights[level] = repeat_blocks(weight_form(node[8:16]))
        if level < levels - 1:
            rows = devices - (devices >> level)
            climb(held, first, devices >> (level + 1), selection_ref, rows, transfer, nodes, rows)
            held, first = nodes, rows

    def turn(at, _):
        for part in range(FAR_TURN):
            columns = pl.ds(pl.multiple_of((at * FAR_TURN + part) * tile, tile), tile)
            target = target_form(own_ref[0:8, columns])
            target = jnp.concatenate([target, jnp.zeros((LANES - 48, tile), BF16)], axis=0)
            pieces = []
            for level in range(levels):
                pieces += kernel_pieces(sources[level], target)
            total = weigh([weights[level] for level in range(levels)], pieces)
            out_ref[:, columns] = (total + near_ref[:, columns]) * scale
        return 0

    lax.fori_loop(0, own_ref.shape[1] // (tile * FAR_TURN), turn, 0)


def far_term(scale, tile, own, near, gathered, selection, transfer):
    devices, _, rank = gathered.shape
    levels = devices.bit_length() - 1
    return pl.pallas_call(
        functools.partial(far_kernel, scale, tile),
        out_shape=jax.ShapeDtypeStruct((8, own.shape[1]), F32),
        in_specs=[VMEM_SPEC] * 5,
        out_specs=VMEM_SPEC,
        scratch_shapes=[
            pltpu.VMEM((devices - 2, 16, rank), F32),
            pltpu.VMEM((levels, rank, LANES), BF16),
            pltpu.VMEM((levels, 16, 2 * rank), BF16),
        ],
        compiler_params=pltpu.CompilerParams(vmem_limit_bytes=32 * 2**20),
        name="far_term",
    )(own, near, gathered, selection, transfer)


def body(coords, right_sides, projection, skel_index, selection, transfer, near_leaf, near_count):
    devices = lax.axis_size("leaf")
    leaves, slots = near_leaf.shape
    leaf = coords.shape[1] // leaves
    scale = 1.0 / (slots * leaf) ** 0.5
    extended, skel_index = extend(coords, right_sides, skel_index)
    chip = swap(extended, "leaf", 0)
    other = swap(extended, "leaf", 1)
    node, own_part = first_step(devices, leaf, extended, projection, skel_index)
    gathered = lax.all_to_all(node, "leaf", 0, 0, tiled=True)
    near = near_term(near_leaf, near_count, own_part, chip, extended, other)
    return far_term(scale, leaf, extended, near, gathered, selection, transfer)


def solution(mesh):
    return jax.shard_map(
        body,
        mesh=mesh,
        in_specs=(
            P(None, "leaf"),
            P(None, "leaf"),
            P("leaf", None),
            P("leaf", None),
            P(),
            P(),
            P("leaf", None),
            P("leaf"),
        ),
        out_specs=P(None, "leaf"),
        check_vma=False,
    )
```

```python
import functools
import math

import jax
import jax.numpy as jnp
from jax import lax
from jax.experimental import pallas as pl
from jax.experimental.pallas import tpu as pltpu
from jax.sharding import PartitionSpec as P

F32 = jnp.float32
BF16 = jnp.bfloat16
LANES = 128
SHIFT = 2.0
NEAR_TURN = 16
FAR_TURN = 32
LEAVES_SELF = 32
ROOT = math.sqrt(math.log2(math.e))
SMEM_SPEC = pl.BlockSpec(memory_space=pltpu.SMEM)
HBM_SPEC = pl.BlockSpec(memory_space=pltpu.HBM)
VMEM_SPEC = pl.BlockSpec(memory_space=pltpu.VMEM)


def swap(value, axis, first):
    count = lax.axis_size(axis)
    pairs = []
    for left in range(first, count - 1, 2):
        pairs += [(left, left + 1), (left + 1, left)]
    return lax.ppermute(value, axis, pairs)


def two_pieces(value):
    high = value.astype(BF16).astype(F32)
    return high, value - high


def three_pieces(value):
    high, rest = two_pieces(value)
    middle, low = two_pieces(rest)
    return high, middle, low


def source_form(extended):
    high, middle, low = three_pieces(extended)
    return jnp.concatenate([high, high, high, middle, middle, low], axis=0).astype(BF16)


def target_form(extended):
    row = lax.broadcasted_iota(jnp.int32, extended.shape, 0)
    below = pltpu.roll(extended, 1, 0)
    swapped = jnp.where(row == 6, 1.0, jnp.where(row == 7, below, extended))
    high, middle, low = three_pieces(swapped)
    return jnp.concatenate([high, middle, low, high, middle, high], axis=0).astype(BF16)


def weight_form(values):
    high, low = two_pieces(values)
    return jnp.concatenate([high, low], axis=0).astype(BF16)


def pick_columns(pieces, index):
    index = jnp.broadcast_to(index, (8, LANES))
    low = index & (LANES - 1)
    high = index >> 7
    result = jnp.take_along_axis(pieces[0], low, axis=1)
    for at in range(1, len(pieces)):
        result = jnp.where(high == at, jnp.take_along_axis(pieces[at], low, axis=1), result)
    return result


def split_block(exponent):
    kernel = jnp.exp2(jnp.minimum(exponent, 0.0))
    high = kernel.astype(BF16)
    return high, (kernel - high.astype(F32)).astype(BF16)


def repeat_blocks(weight):
    pieces = []
    for first in range(0, weight.shape[1], LANES):
        pieces += [weight[:, first:first + LANES]] * 2
    return jnp.concatenate(pieces, axis=1)


def kernel_term(source, target, weight):
    total = None
    for first in range(0, source.shape[0], LANES):
        high, low = split_block(jnp.dot(source[first:first + LANES], target, preferred_element_type=F32))
        both = jnp.concatenate([high, low], axis=0)
        term = jnp.dot(weight[:, 2 * first:2 * (first + LANES)], both, preferred_element_type=F32)
        total = term if total is None else total + term
    return total


def kernel_pieces(source, target):
    pieces = []
    for first in range(0, source.shape[0], LANES):
        pieces += split_block(jnp.dot(source[first:first + LANES], target, preferred_element_type=F32))
    return pieces


def weigh(weights, pieces):
    weights = jnp.concatenate(weights, axis=1)
    return fold(jnp.dot(weights, jnp.concatenate(pieces, axis=0), preferred_element_type=F32))


def fold(pieces):
    return pieces[:8] + pieces[8:]


def add_norm(ref):
    centred = ref[0:6, :]
    ref[6:7, :] = -0.5 * jnp.sum(centred * centred, axis=0, keepdims=True)
    ref[7:8, :] = jnp.ones((1, centred.shape[1]), F32)


def packed_parts(points):
    quarter = points // 4
    return slice(points, points + 3 * quarter), [
        slice(points + part * quarter, points + (part + 1) * quarter) for part in range(3)
    ]


def extend_kernel(coords_ref, right_ref, index_hbm, out_ref, packed_ref, index_ref, held, sems):
    rows, points = held.shape
    copies = [
        pltpu.make_async_copy(coords_ref, held, sems.at[0]),
        pltpu.make_async_copy(right_ref, out_ref.at[pl.ds(8, 8)], sems.at[1]),
        pltpu.make_async_copy(right_ref, packed_ref.at[:, pl.ds(0, points)], sems.at[2]),
        pltpu.make_async_copy(index_hbm, index_ref, sems.at[3]),
    ]
    for copy in copies:
        copy.start()
    copies[0].wait()
    centred = (held[...] - SHIFT) * ROOT
    out_ref[0:rows, :] = centred
    front, parts = packed_parts(points)
    last = 3 * (points // 4)
    packed_ref[0:rows, front] = centred[:, :last]
    for part, columns in enumerate(parts):
        packed_ref[rows:rows + 2, columns] = out_ref[2 * part:2 * part + 2, last:]
    out_ref[rows:rows + 1, :] = -0.5 * jnp.sum(centred * centred, axis=0, keepdims=True)
    out_ref[rows + 1:rows + 2, :] = jnp.ones((1, points), F32)
    for copy in copies[1:]:
        copy.wait()


def extend(coords, right_sides, skel_index):
    rows, points = coords.shape
    return pl.pallas_call(
        extend_kernel,
        out_shape=(
            pltpu.VMEM((16, points), F32),
            pltpu.VMEM((8, points + 3 * (points // 4)), F32),
            pltpu.VMEM(skel_index.shape, jnp.int32),
        ),
        in_specs=[HBM_SPEC] * 3,
        out_specs=(VMEM_SPEC,) * 3,
        scratch_shapes=[pltpu.VMEM((rows, points), F32), pltpu.SemaphoreType.DMA((4,))],
        compiler_params=pltpu.CompilerParams(vmem_limit_bytes=58 * 2**20),
        name="extend",
    )(coords, right_sides, skel_index)


def first_kernel(leaf, x_ref, proj_ref, index_ref, node_ref, self_ref, held, sources, weights, targets, sems):
    chunks = held.shape[0]
    chunk, rank = held.shape[1:]
    points = x_ref.shape[1]
    copies = [
        pltpu.make_async_copy(proj_ref.at[pl.ds(at * chunk, chunk)], held.at[at], sems.at[at]) for at in range(chunks)
    ]
    for copy in copies:
        copy.start()
    for half in range(rank // LANES):
        lanes = slice(half * LANES, (half + 1) * LANES)
        pieces = [x_ref[0:8, at * LANES:(at + 1) * LANES] for at in range(points // LANES)]
        columns = pick_columns(pieces, index_ref[:, lanes])
        for copy in range(node_ref.shape[0]):
            node_ref[copy, 0:8, lanes] = columns
    wide = 8 * leaf

    def prepare(at, _):
        columns = pl.ds(pl.multiple_of(at * wide, wide), wide)
        sources[:, columns] = source_form(x_ref[0:8, columns])
        twice = pl.ds(pl.multiple_of(at * 2 * wide, wide), 2 * wide)
        weights[:, twice] = repeat_blocks(weight_form(x_ref[8:16, columns]))
        targets[:, columns] = target_form(x_ref[0:8, columns])
        return 0

    def turn(at, _):
        for part in range(LEAVES_SELF):
            columns = pl.ds(pl.multiple_of((at * LEAVES_SELF + part) * leaf, leaf), leaf)
            twice = pl.ds(pl.multiple_of((at * LEAVES_SELF + part) * 2 * leaf, leaf), 2 * leaf)
            self_ref[:, columns] = fold(kernel_term(sources[:, columns].T, targets[:, columns], weights[:, twice]))
        return 0

    lax.fori_loop(0, points // wide, prepare, 0)
    lax.fori_loop(0, points // (leaf * LEAVES_SELF), turn, 0)
    total = jnp.zeros((8, rank), F32)
    for at in range(chunks):
        x_high, x_low = two_pieces(x_ref[8:16, at * chunk:(at + 1) * chunk])
        left = jnp.concatenate([x_high, x_low], axis=0).astype(BF16)
        copies[at].wait()
        p_high, p_low = two_pieces(held[at])
        both = jnp.dot(left, p_high.astype(BF16), preferred_element_type=F32)
        part = jnp.dot(left, p_low.astype(BF16), preferred_element_type=F32)
        total += both[:8] + both[8:] + part[:8]
    for copy in range(node_ref.shape[0]):
        node_ref[copy, 8:16, :] = total


def first_step(copies, leaf, extended, projection, skel_index):
    points, rank = projection.shape
    chunks = 8
    return pl.pallas_call(
        functools.partial(first_kernel, leaf),
        out_shape=(
            jax.ShapeDtypeStruct((copies, 16, rank), F32),
            jax.ShapeDtypeStruct((8, points), F32),
        ),
        in_specs=[VMEM_SPEC, HBM_SPEC, VMEM_SPEC],
        out_specs=(VMEM_SPEC, VMEM_SPEC),
        scratch_shapes=[
            pltpu.VMEM((chunks, points // chunks, rank), F32),
            pltpu.VMEM((48, points), BF16),
            pltpu.VMEM((16, 2 * points), BF16),
            pltpu.VMEM((48, points), BF16),
            pltpu.SemaphoreType.DMA((chunks,)),
        ],
        compiler_params=pltpu.CompilerParams(vmem_limit_bytes=50 * 2**20),
        name="first_step",
    )(extended, projection, skel_index)


def climb(source, first, count, selection, rows, transfer, target, offset):
    rank = transfer[0].shape[1]
    t_high, t_low = transfer
    joined = jnp.concatenate(
        [
            jnp.concatenate([source[first + 2 * m + side, 8:16, :] for m in range(count)], axis=0)
            for side in range(2)
        ],
        axis=1,
    )
    high, low = two_pieces(joined)
    left = jnp.concatenate([high, low], axis=0).astype(BF16)
    both = jnp.dot(left, t_high, preferred_element_type=F32)
    part = jnp.dot(left, t_low, preferred_element_type=F32)
    moved = both[:8 * count] + both[8 * count:] + part[:8 * count]
    for m in range(count):
        target[offset + m, 8:16, :] = moved[m * 8:(m + 1) * 8, :]
        pieces = [
            source[first + 2 * m + side, 0:8, at * LANES:(at + 1) * LANES]
            for side in range(2)
            for at in range(rank // LANES)
        ]
        picked = selection[pl.ds(rows + m, 1), :]
        for half in range(rank // LANES):
            lanes = slice(half * LANES, (half + 1) * LANES)
            target[offset + m, 0:8, lanes] = pick_columns(pieces, picked[:, lanes])


def split_transfer(transfer_ref):
    t_high, t_low = two_pieces(transfer_ref[...])
    return t_high.astype(BF16), t_low.astype(BF16)


def near_kernel(near_ref, count_ref, self_ref, chip_ref, own_ref, other_ref, out_ref, sources, weights, targets, unpacked):
    leaves, slots = near_ref.shape
    points = own_ref.shape[1]
    leaf = points // leaves
    own_index = lax.axis_index("leaf")
    even = own_index % 2 == 0
    first_leaf = own_index * leaves
    wide = 8 * leaf

    front, parts = packed_parts(points)
    last = 3 * (points // 4)
    for side, ref in enumerate((chip_ref, other_ref)):
        target = unpacked.at[side]
        target[0:6, 0:last] = ref[0:6, front]
        for part, columns in enumerate(parts):
            target[2 * part:2 * part + 2, last:] = ref[6:8, columns]
        add_norm(target)

    def prepare(at, _):
        columns = pl.ds(pl.multiple_of(at * wide, wide), wide)
        for part, (coords, values) in enumerate(
            ((unpacked.at[0], chip_ref), (own_ref, own_ref.at[pl.ds(8, 8)]), (unpacked.at[1], other_ref))
        ):
            window = pl.ds(pl.multiple_of(part * points + at * wide, wide), wide)
            sources[:, window] = source_form(coords[0:8, columns])
            twice = pl.ds(pl.multiple_of(2 * (part * points + at * wide), wide), 2 * wide)
            weights[:, twice] = repeat_blocks(weight_form(values[0:8, columns]))
        targets[:, columns] = target_form(own_ref[0:8, columns])
        return 0

    lax.fori_loop(0, points // wide, prepare, 0)

    def window_place(offset):
        below, above = offset < 0, offset >= leaves
        left = jnp.where(even, 2, 0)
        part = jnp.where(below, left, jnp.where(above, 2 - left, 1))
        local = jnp.where(below, offset + leaves, jnp.where(above, offset - leaves, offset))
        return part * leaves + jnp.clip(local, 0, leaves - 1)

    def one_leaf(at, live_slots):
        columns = pl.ds(pl.multiple_of(at * leaf, leaf), leaf)
        target = targets[:, columns]
        held, pieces = [], []
        for slot in range(1, live_slots):
            place = window_place(near_ref[at, slot] - first_leaf)
            window = pl.ds(pl.multiple_of(place * leaf, leaf), leaf)
            weight = weights[:, pl.ds(pl.multiple_of(place * 2 * leaf, leaf), 2 * leaf)]
            held.append(jnp.where(slot < count_ref[at], weight, jnp.zeros_like(weight)))
            pieces += kernel_pieces(sources[:, window].T, target)
        out_ref[:, columns] = self_ref[:, columns] + weigh(held, pieces)

    def turn(at, _):
        most = count_ref[NEAR_TURN * at]
        for leaf_at in range(1, NEAR_TURN):
            most = jnp.maximum(most, count_ref[NEAR_TURN * at + leaf_at])
        heavy = most > slots // 2

        @pl.when(heavy)
        def _():
            for leaf_at in range(NEAR_TURN):
                one_leaf(NEAR_TURN * at + leaf_at, slots)

        @pl.when(jnp.logical_not(heavy))
        def _():
            for leaf_at in range(NEAR_TURN):
                one_leaf(NEAR_TURN * at + leaf_at, slots // 2)

        return 0

    lax.fori_loop(0, leaves // NEAR_TURN, turn, 0)


def near_term(near_leaf, near_count, own_part, chip, own, other):
    leaves, slots = near_leaf.shape
    points = own.shape[1]
    entries = leaves * slots * (points // leaves) ** 2
    return pl.pallas_call(
        near_kernel,
        out_shape=jax.ShapeDtypeStruct((8, points), F32),
        in_specs=[SMEM_SPEC] * 2 + [VMEM_SPEC] * 4,
        out_specs=VMEM_SPEC,
        scratch_shapes=[
            pltpu.VMEM((48, 3 * points), BF16),
            pltpu.VMEM((16, 6 * points), BF16),
            pltpu.VMEM((48, points), BF16),
            pltpu.VMEM((2, 8, points), F32),
        ],
        cost_estimate=pl.CostEstimate(flops=1000 * entries, bytes_accessed=4 * 64 * points, transcendentals=entries),
        compiler_params=pltpu.CompilerParams(vmem_limit_bytes=32 * 2**20),
        name="near_term",
    )(near_leaf, near_count, own_part, chip, own, other)


def far_kernel(scale, tile, own_ref, near_ref, gathered_ref, selection_ref, transfer_ref, out_ref, nodes, sources, weights):
    devices = gathered_ref.shape[0]
    levels = devices.bit_length() - 1
    own_index = lax.axis_index("leaf")
    transfer = split_transfer(transfer_ref)
    rank = transfer_ref.shape[1]
    held, first = gathered_ref, 0
    for level in range(levels):
        node = held[first + ((own_index >> level) ^ 1)]
        form = source_form(node[0:8])
        sources[level] = jnp.concatenate([form, jnp.zeros((LANES - 48, rank), BF16)], axis=0).T
        weights[level] = repeat_blocks(weight_form(node[8:16]))
        if level < levels - 1:
            rows = devices - (devices >> level)
            climb(held, first, devices >> (level + 1), selection_ref, rows, transfer, nodes, rows)
            held, first = nodes, rows

    def turn(at, _):
        for part in range(FAR_TURN):
            columns = pl.ds(pl.multiple_of((at * FAR_TURN + part) * tile, tile), tile)
            target = target_form(own_ref[0:8, columns])
            target = jnp.concatenate([target, jnp.zeros((LANES - 48, tile), BF16)], axis=0)
            pieces = []
            for level in range(levels):
                pieces += kernel_pieces(sources[level], target)
            total = weigh([weights[level] for level in range(levels)], pieces)
            out_ref[:, columns] = (total + near_ref[:, columns]) * scale
        return 0

    lax.fori_loop(0, own_ref.shape[1] // (tile * FAR_TURN), turn, 0)


def far_term(scale, tile, own, near, gathered, selection, transfer):
    devices, _, rank = gathered.shape
    levels = devices.bit_length() - 1
    return pl.pallas_call(
        functools.partial(far_kernel, scale, tile),
        out_shape=jax.ShapeDtypeStruct((8, own.shape[1]), F32),
        in_specs=[VMEM_SPEC] * 5,
        out_specs=VMEM_SPEC,
        scratch_shapes=[
            pltpu.VMEM((devices - 2, 16, rank), F32),
            pltpu.VMEM((levels, rank, LANES), BF16),
            pltpu.VMEM((levels, 16, 2 * rank), BF16),
        ],
        compiler_params=pltpu.CompilerParams(vmem_limit_bytes=32 * 2**20),
        name="far_term",
    )(own, near, gathered, selection, transfer)


def body(coords, right_sides, projection, skel_index, selection, transfer, near_leaf, near_count):
    devices = lax.axis_size("leaf")
    leaves, slots = near_leaf.shape
    leaf = coords.shape[1] // leaves
    scale = 1.0 / (slots * leaf) ** 0.5
    extended, packed, skel_index = extend(coords, right_sides, skel_index)
    chip = swap(packed, "leaf", 0)
    other = swap(packed, "leaf", 1)
    node, own_part = first_step(devices, leaf, extended, projection, skel_index)
    gathered = lax.all_to_all(node, "leaf", 0, 0, tiled=True)
    near = near_term(near_leaf, near_count, own_part, chip, extended, other)
    return far_term(scale, leaf, extended, near, gathered, selection, transfer)


def solution(mesh):
    return jax.shard_map(
        body,
        mesh=mesh,
        in_specs=(
            P(None, "leaf"),
            P(None, "leaf"),
            P("leaf", None),
            P("leaf", None),
            P(),
            P(),
            P("leaf", None),
            P("leaf"),
        ),
        out_specs=P(None, "leaf"),
        check_vma=False,
    )
```

```python
import functools
import math

import jax
import jax.numpy as jnp
from jax import lax
from jax.experimental import pallas as pl
from jax.experimental.pallas import tpu as pltpu
from jax.sharding import PartitionSpec as P

F32 = jnp.float32
BF16 = jnp.bfloat16
LANES = 128
SHIFT = 2.0
NEAR_TURN = 16
FAR_TURN = 32
LEAVES_SELF = 16
ROOT = math.sqrt(math.log2(math.e))
SMEM_SPEC = pl.BlockSpec(memory_space=pltpu.SMEM)
HBM_SPEC = pl.BlockSpec(memory_space=pltpu.HBM)
VMEM_SPEC = pl.BlockSpec(memory_space=pltpu.VMEM)


def swap(value, axis, first):
    count = lax.axis_size(axis)
    pairs = []
    for left in range(first, count - 1, 2):
        pairs += [(left, left + 1), (left + 1, left)]
    return lax.ppermute(value, axis, pairs)


def two_pieces(value):
    high = value.astype(BF16).astype(F32)
    return high, value - high


def three_pieces(value):
    high, rest = two_pieces(value)
    middle, low = two_pieces(rest)
    return high, middle, low


def source_form(extended):
    high, middle, low = three_pieces(extended)
    return jnp.concatenate([high, high, high, middle, middle, low], axis=0).astype(BF16)


def target_form(extended):
    row = lax.broadcasted_iota(jnp.int32, extended.shape, 0)
    below = pltpu.roll(extended, 1, 0)
    swapped = jnp.where(row == 6, 1.0, jnp.where(row == 7, below, extended))
    high, middle, low = three_pieces(swapped)
    return jnp.concatenate([high, middle, low, high, middle, high], axis=0).astype(BF16)


def weight_form(values):
    high, low = two_pieces(values)
    return jnp.concatenate([high, low], axis=0).astype(BF16)


def pick_columns(pieces, index):
    index = jnp.broadcast_to(index, (8, LANES))
    low = index & (LANES - 1)
    high = index >> 7
    result = jnp.take_along_axis(pieces[0], low, axis=1)
    for at in range(1, len(pieces)):
        result = jnp.where(high == at, jnp.take_along_axis(pieces[at], low, axis=1), result)
    return result


def split_block(exponent):
    kernel = jnp.exp2(jnp.minimum(exponent, 0.0))
    high = kernel.astype(BF16)
    return high, (kernel - high.astype(F32)).astype(BF16)


def repeat_blocks(weight):
    pieces = []
    for first in range(0, weight.shape[1], LANES):
        pieces += [weight[:, first:first + LANES]] * 2
    return jnp.concatenate(pieces, axis=1)


def kernel_term(source, target, weight):
    total = None
    for first in range(0, source.shape[0], LANES):
        high, low = split_block(jnp.dot(source[first:first + LANES], target, preferred_element_type=F32))
        both = jnp.concatenate([high, low], axis=0)
        term = jnp.dot(weight[:, 2 * first:2 * (first + LANES)], both, preferred_element_type=F32)
        total = term if total is None else total + term
    return total


def kernel_pieces(source, target, rows, chunk):
    pieces = []
    for first in range(0, source.shape[0], rows):
        split = [
            split_block(jnp.dot(source[at:at + chunk], target, preferred_element_type=F32))
            for at in range(first, first + rows, chunk)
        ]
        pieces += [high for high, _ in split] + [low for _, low in split]
    return pieces


def weigh(weights, pieces):
    weights = jnp.concatenate(weights, axis=1)
    return fold(jnp.dot(weights, jnp.concatenate(pieces, axis=0), preferred_element_type=F32))


def fold(pieces):
    return pieces[:8] + pieces[8:]


def add_norm(ref):
    centred = ref[0:6, :]
    ref[6:7, :] = -0.5 * jnp.sum(centred * centred, axis=0, keepdims=True)
    ref[7:8, :] = jnp.ones((1, centred.shape[1]), F32)


def packed_parts(points):
    quarter = points // 4
    return slice(points, points + 3 * quarter), [
        slice(points + part * quarter, points + (part + 1) * quarter) for part in range(3)
    ]


def extend_kernel(coords_ref, right_ref, index_hbm, out_ref, packed_ref, index_ref, held, sems):
    rows, points = held.shape
    copies = [
        pltpu.make_async_copy(coords_ref, held, sems.at[0]),
        pltpu.make_async_copy(right_ref, out_ref.at[pl.ds(8, 8)], sems.at[1]),
        pltpu.make_async_copy(right_ref, packed_ref.at[:, pl.ds(0, points)], sems.at[2]),
        pltpu.make_async_copy(index_hbm, index_ref, sems.at[3]),
    ]
    for copy in copies:
        copy.start()
    copies[0].wait()
    centred = (held[...] - SHIFT) * ROOT
    out_ref[0:rows, :] = centred
    front, parts = packed_parts(points)
    last = 3 * (points // 4)
    packed_ref[0:rows, front] = centred[:, :last]
    for part, columns in enumerate(parts):
        packed_ref[rows:rows + 2, columns] = out_ref[2 * part:2 * part + 2, last:]
    out_ref[rows:rows + 1, :] = -0.5 * jnp.sum(centred * centred, axis=0, keepdims=True)
    out_ref[rows + 1:rows + 2, :] = jnp.ones((1, points), F32)
    for copy in copies[1:]:
        copy.wait()


def extend(coords, right_sides, skel_index):
    rows, points = coords.shape
    return pl.pallas_call(
        extend_kernel,
        out_shape=(
            pltpu.VMEM((16, points), F32),
            pltpu.VMEM((8, points + 3 * (points // 4)), F32),
            pltpu.VMEM(skel_index.shape, jnp.int32),
        ),
        in_specs=[HBM_SPEC] * 3,
        out_specs=(VMEM_SPEC,) * 3,
        scratch_shapes=[pltpu.VMEM((rows, points), F32), pltpu.SemaphoreType.DMA((4,))],
        compiler_params=pltpu.CompilerParams(vmem_limit_bytes=58 * 2**20),
        name="extend",
    )(coords, right_sides, skel_index)


def first_kernel(leaf, x_ref, proj_ref, index_ref, node_ref, self_ref, held, sources, weights, targets, sems):
    chunks = held.shape[0]
    chunk, rank = held.shape[1:]
    points = x_ref.shape[1]
    copies = [
        pltpu.make_async_copy(proj_ref.at[pl.ds(at * chunk, chunk)], held.at[at], sems.at[at]) for at in range(chunks)
    ]
    for copy in copies:
        copy.start()
    for half in range(rank // LANES):
        lanes = slice(half * LANES, (half + 1) * LANES)
        pieces = [x_ref[0:8, at * LANES:(at + 1) * LANES] for at in range(points // LANES)]
        columns = pick_columns(pieces, index_ref[:, lanes])
        for copy in range(node_ref.shape[0]):
            node_ref[copy, 0:8, lanes] = columns
    wide = 8 * leaf

    def prepare(at, _):
        columns = pl.ds(pl.multiple_of(at * wide, wide), wide)
        sources[:, columns] = source_form(x_ref[0:8, columns])
        twice = pl.ds(pl.multiple_of(at * 2 * wide, wide), 2 * wide)
        weights[:, twice] = repeat_blocks(weight_form(x_ref[8:16, columns]))
        targets[:, columns] = target_form(x_ref[0:8, columns])
        return 0

    def turn(at, _):
        for part in range(LEAVES_SELF):
            columns = pl.ds(pl.multiple_of((at * LEAVES_SELF + part) * leaf, leaf), leaf)
            twice = pl.ds(pl.multiple_of((at * LEAVES_SELF + part) * 2 * leaf, leaf), 2 * leaf)
            self_ref[:, columns] = fold(kernel_term(sources[:, columns].T, targets[:, columns], weights[:, twice]))
        return 0

    lax.fori_loop(0, points // wide, prepare, 0)
    lax.fori_loop(0, points // (leaf * LEAVES_SELF), turn, 0)
    total = jnp.zeros((8, rank), F32)
    for at in range(chunks):
        x_high, x_low = two_pieces(x_ref[8:16, at * chunk:(at + 1) * chunk])
        left = jnp.concatenate([x_high, x_low], axis=0).astype(BF16)
        copies[at].wait()
        p_high, p_low = two_pieces(held[at])
        both = jnp.dot(left, p_high.astype(BF16), preferred_element_type=F32)
        part = jnp.dot(left, p_low.astype(BF16), preferred_element_type=F32)
        total += both[:8] + both[8:] + part[:8]
    for copy in range(node_ref.shape[0]):
        node_ref[copy, 8:16, :] = total


def first_step(copies, leaf, extended, projection, skel_index):
    points, rank = projection.shape
    chunks = 8
    return pl.pallas_call(
        functools.partial(first_kernel, leaf),
        out_shape=(
            jax.ShapeDtypeStruct((copies, 16, rank), F32),
            jax.ShapeDtypeStruct((8, points), F32),
        ),
        in_specs=[VMEM_SPEC, HBM_SPEC, VMEM_SPEC],
        out_specs=(VMEM_SPEC, VMEM_SPEC),
        scratch_shapes=[
            pltpu.VMEM((chunks, points // chunks, rank), F32),
            pltpu.VMEM((48, points), BF16),
            pltpu.VMEM((16, 2 * points), BF16),
            pltpu.VMEM((48, points), BF16),
            pltpu.SemaphoreType.DMA((chunks,)),
        ],
        compiler_params=pltpu.CompilerParams(vmem_limit_bytes=50 * 2**20),
        name="first_step",
    )(extended, projection, skel_index)


def climb(source, first, count, selection, rows, transfer, target, offset):
    rank = transfer[0].shape[1]
    t_high, t_low = transfer
    joined = jnp.concatenate(
        [
            jnp.concatenate([source[first + 2 * m + side, 8:16, :] for m in range(count)], axis=0)
            for side in range(2)
        ],
        axis=1,
    )
    high, low = two_pieces(joined)
    left = jnp.concatenate([high, low], axis=0).astype(BF16)
    both = jnp.dot(left, t_high, preferred_element_type=F32)
    part = jnp.dot(left, t_low, preferred_element_type=F32)
    moved = both[:8 * count] + both[8 * count:] + part[:8 * count]
    for m in range(count):
        target[offset + m, 8:16, :] = moved[m * 8:(m + 1) * 8, :]
        pieces = [
            source[first + 2 * m + side, 0:8, at * LANES:(at + 1) * LANES]
            for side in range(2)
            for at in range(rank // LANES)
        ]
        picked = selection[pl.ds(rows + m, 1), :]
        for half in range(rank // LANES):
            lanes = slice(half * LANES, (half + 1) * LANES)
            target[offset + m, 0:8, lanes] = pick_columns(pieces, picked[:, lanes])


def split_transfer(transfer_ref):
    t_high, t_low = two_pieces(transfer_ref[...])
    return t_high.astype(BF16), t_low.astype(BF16)


def near_kernel(near_ref, count_ref, self_ref, chip_ref, own_ref, other_ref, out_ref, sources, weights, targets, unpacked):
    leaves, slots = near_ref.shape
    points = own_ref.shape[1]
    leaf = points // leaves
    own_index = lax.axis_index("leaf")
    even = own_index % 2 == 0
    first_leaf = own_index * leaves
    wide = 8 * leaf

    front, parts = packed_parts(points)
    last = 3 * (points // 4)
    unpacked[0:6, 0:last] = other_ref[0:6, front]
    for part, columns in enumerate(parts):
        unpacked[2 * part:2 * part + 2, last:] = other_ref[6:8, columns]
    add_norm(unpacked)

    def prepare(at, _):
        columns = pl.ds(pl.multiple_of(at * wide, wide), wide)
        for part, (coords, values) in enumerate(
            ((chip_ref, chip_ref.at[pl.ds(8, 8)]), (own_ref, own_ref.at[pl.ds(8, 8)]), (unpacked, other_ref))
        ):
            window = pl.ds(pl.multiple_of(part * points + at * wide, wide), wide)
            sources[:, window] = source_form(coords[0:8, columns])
            twice = pl.ds(pl.multiple_of(2 * (part * points + at * wide), wide), 2 * wide)
            weights[:, twice] = repeat_blocks(weight_form(values[0:8, columns]))
        targets[:, columns] = target_form(own_ref[0:8, columns])
        return 0

    lax.fori_loop(0, points // wide, prepare, 0)

    def window_place(offset):
        below, above = offset < 0, offset >= leaves
        left = jnp.where(even, 2, 0)
        part = jnp.where(below, left, jnp.where(above, 2 - left, 1))
        local = jnp.where(below, offset + leaves, jnp.where(above, offset - leaves, offset))
        return part * leaves + jnp.clip(local, 0, leaves - 1)

    def one_leaf(at, live_slots):
        columns = pl.ds(pl.multiple_of(at * leaf, leaf), leaf)
        target = targets[:, columns]
        held, pieces = [], []
        for slot in range(1, live_slots):
            place = window_place(near_ref[at, slot] - first_leaf)
            window = pl.ds(pl.multiple_of(place * leaf, leaf), leaf)
            weight = weights[:, pl.ds(pl.multiple_of(place * 2 * leaf, leaf), 2 * leaf)]
            held.append(jnp.where(slot < count_ref[at], weight, jnp.zeros_like(weight)))
            pieces += kernel_pieces(sources[:, window].T, target, LANES, 64)
        out_ref[:, columns] = self_ref[:, columns] + weigh(held, pieces)

    def turn(at, _):
        most = count_ref[NEAR_TURN * at]
        for leaf_at in range(1, NEAR_TURN):
            most = jnp.maximum(most, count_ref[NEAR_TURN * at + leaf_at])
        heavy = most > slots // 2

        @pl.when(heavy)
        def _():
            for leaf_at in range(NEAR_TURN):
                one_leaf(NEAR_TURN * at + leaf_at, slots)

        @pl.when(jnp.logical_not(heavy))
        def _():
            for leaf_at in range(NEAR_TURN):
                one_leaf(NEAR_TURN * at + leaf_at, slots // 2)

        return 0

    lax.fori_loop(0, leaves // NEAR_TURN, turn, 0)


def near_term(near_leaf, near_count, own_part, chip, own, other):
    leaves, slots = near_leaf.shape
    points = own.shape[1]
    entries = leaves * slots * (points // leaves) ** 2
    return pl.pallas_call(
        near_kernel,
        out_shape=jax.ShapeDtypeStruct((8, points), F32),
        in_specs=[SMEM_SPEC] * 2 + [VMEM_SPEC] * 4,
        out_specs=VMEM_SPEC,
        scratch_shapes=[
            pltpu.VMEM((48, 3 * points), BF16),
            pltpu.VMEM((16, 6 * points), BF16),
            pltpu.VMEM((48, points), BF16),
            pltpu.VMEM((8, points), F32),
        ],
        cost_estimate=pl.CostEstimate(flops=1000 * entries, bytes_accessed=4 * 64 * points, transcendentals=entries),
        compiler_params=pltpu.CompilerParams(vmem_limit_bytes=32 * 2**20),
        name="near_term",
    )(near_leaf, near_count, own_part, chip, own, other)


def far_kernel(scale, tile, own_ref, near_ref, gathered_ref, selection_ref, transfer_ref, out_ref, nodes, sources, weights):
    devices = gathered_ref.shape[0]
    levels = devices.bit_length() - 1
    own_index = lax.axis_index("leaf")
    transfer = split_transfer(transfer_ref)
    rank = transfer_ref.shape[1]
    held, first = gathered_ref, 0
    for level in range(levels):
        node = held[first + ((own_index >> level) ^ 1)]
        form = source_form(node[0:8])
        sources[level] = jnp.concatenate([form, jnp.zeros((LANES - 48, rank), BF16)], axis=0).T
        form = weight_form(node[8:16])
        weights[level] = jnp.concatenate([form, form], axis=1)
        if level < levels - 1:
            rows = devices - (devices >> level)
            climb(held, first, devices >> (level + 1), selection_ref, rows, transfer, nodes, rows)
            held, first = nodes, rows

    def turn(at, _):
        for part in range(FAR_TURN):
            columns = pl.ds(pl.multiple_of((at * FAR_TURN + part) * tile, tile), tile)
            target = target_form(own_ref[0:8, columns])
            target = jnp.concatenate([target, jnp.zeros((LANES - 48, tile), BF16)], axis=0)
            pieces = []
            for level in range(levels):
                pieces += kernel_pieces(sources[level], target, rank, rank)
            total = weigh([weights[level] for level in range(levels)], pieces)
            out_ref[:, columns] = (total + near_ref[:, columns]) * scale
        return 0

    lax.fori_loop(0, own_ref.shape[1] // (tile * FAR_TURN), turn, 0)


def far_term(scale, tile, own, near, gathered, selection, transfer):
    devices, _, rank = gathered.shape
    levels = devices.bit_length() - 1
    return pl.pallas_call(
        functools.partial(far_kernel, scale, tile),
        out_shape=jax.ShapeDtypeStruct((8, own.shape[1]), F32),
        in_specs=[VMEM_SPEC] * 5,
        out_specs=VMEM_SPEC,
        scratch_shapes=[
            pltpu.VMEM((devices - 2, 16, rank), F32),
            pltpu.VMEM((levels, rank, LANES), BF16),
            pltpu.VMEM((levels, 16, 2 * rank), BF16),
        ],
        compiler_params=pltpu.CompilerParams(vmem_limit_bytes=32 * 2**20),
        name="far_term",
    )(own, near, gathered, selection, transfer)


def body(coords, right_sides, projection, skel_index, selection, transfer, near_leaf, near_count):
    devices = lax.axis_size("leaf")
    leaves, slots = near_leaf.shape
    leaf = coords.shape[1] // leaves
    scale = 1.0 / (slots * leaf) ** 0.5
    extended, packed, skel_index = extend(coords, right_sides, skel_index)
    chip = swap(extended, "leaf", 0)
    other = swap(packed, "leaf", 1)
    node, own_part = first_step(devices, leaf, extended, projection, skel_index)
    gathered = lax.all_to_all(node, "leaf", 0, 0, tiled=True)
    near = near_term(near_leaf, near_count, own_part, chip, extended, other)
    return far_term(scale, leaf, extended, near, gathered, selection, transfer)


def solution(mesh):
    return jax.shard_map(
        body,
        mesh=mesh,
        in_specs=(
            P(None, "leaf"),
            P(None, "leaf"),
            P("leaf", None),
            P("leaf", None),
            P(),
            P(),
            P("leaf", None),
            P("leaf"),
        ),
        out_specs=P(None, "leaf"),
        check_vma=False,
    )
```

```python
import functools
import math

import jax
import jax.numpy as jnp
from jax import lax
from jax.experimental import pallas as pl
from jax.experimental.pallas import tpu as pltpu
from jax.sharding import PartitionSpec as P

F32 = jnp.float32
BF16 = jnp.bfloat16
LANES = 128
SHIFT = 2.0
NEAR_TURN = 16
FAR_TURN = 32
LEAVES_SELF = 16
ROOT = math.sqrt(math.log2(math.e))
SMEM_SPEC = pl.BlockSpec(memory_space=pltpu.SMEM)
HBM_SPEC = pl.BlockSpec(memory_space=pltpu.HBM)
VMEM_SPEC = pl.BlockSpec(memory_space=pltpu.VMEM)


def swap(value, axis, first):
    count = lax.axis_size(axis)
    pairs = []
    for left in range(first, count - 1, 2):
        pairs += [(left, left + 1), (left + 1, left)]
    return lax.ppermute(value, axis, pairs)


def two_pieces(value):
    high = value.astype(BF16).astype(F32)
    return high, value - high


def three_pieces(value):
    high, rest = two_pieces(value)
    middle, low = two_pieces(rest)
    return high, middle, low


def source_form(extended):
    high, middle, low = three_pieces(extended)
    return jnp.concatenate([high, high, high, middle, middle, low], axis=0).astype(BF16)


def target_form(extended):
    row = lax.broadcasted_iota(jnp.int32, extended.shape, 0)
    below = pltpu.roll(extended, 1, 0)
    swapped = jnp.where(row == 6, 1.0, jnp.where(row == 7, below, extended))
    high, middle, low = three_pieces(swapped)
    return jnp.concatenate([high, middle, low, high, middle, high], axis=0).astype(BF16)


def weight_form(values):
    high, low = two_pieces(values)
    return jnp.concatenate([high, low], axis=0).astype(BF16)


def pick_columns(pieces, index):
    index = jnp.broadcast_to(index, (8, LANES))
    low = index & (LANES - 1)
    high = index >> 7
    result = jnp.take_along_axis(pieces[0], low, axis=1)
    for at in range(1, len(pieces)):
        result = jnp.where(high == at, jnp.take_along_axis(pieces[at], low, axis=1), result)
    return result


def split_block(exponent):
    kernel = jnp.exp2(jnp.minimum(exponent, 0.0))
    high = kernel.astype(BF16)
    return high, (kernel - high.astype(F32)).astype(BF16)


def repeat_blocks(weight):
    pieces = []
    for first in range(0, weight.shape[1], LANES):
        pieces += [weight[:, first:first + LANES]] * 2
    return jnp.concatenate(pieces, axis=1)


def kernel_term(source, target, weight):
    total = None
    for first in range(0, source.shape[0], LANES):
        high, low = split_block(jnp.dot(source[first:first + LANES], target, preferred_element_type=F32))
        both = jnp.concatenate([high, low], axis=0)
        term = jnp.dot(weight[:, 2 * first:2 * (first + LANES)], both, preferred_element_type=F32)
        total = term if total is None else total + term
    return total


def kernel_pieces(source, target, rows, chunk):
    pieces = []
    for first in range(0, source.shape[0], rows):
        split = [
            split_block(jnp.dot(source[at:at + chunk], target, preferred_element_type=F32))
            for at in range(first, first + rows, chunk)
        ]
        pieces += [high for high, _ in split] + [low for _, low in split]
    return pieces


def weigh(weights, pieces):
    weights = jnp.concatenate(weights, axis=1)
    return fold(jnp.dot(weights, jnp.concatenate(pieces, axis=0), preferred_element_type=F32))


def fold(pieces):
    return pieces[:8] + pieces[8:]


def add_norm(ref):
    centred = ref[0:6, :]
    ref[6:7, :] = -0.5 * jnp.sum(centred * centred, axis=0, keepdims=True)
    ref[7:8, :] = jnp.ones((1, centred.shape[1]), F32)


def packed_parts(points):
    quarter = points // 4
    return slice(points, points + 3 * quarter), [
        slice(points + part * quarter, points + (part + 1) * quarter) for part in range(3)
    ]


def extend_kernel(coords_ref, right_ref, index_hbm, out_ref, packed_ref, index_ref, held, sems):
    rows, points = held.shape
    copies = [
        pltpu.make_async_copy(coords_ref, held, sems.at[0]),
        pltpu.make_async_copy(right_ref, out_ref.at[pl.ds(8, 8)], sems.at[1]),
        pltpu.make_async_copy(right_ref, packed_ref.at[:, pl.ds(0, points)], sems.at[2]),
        pltpu.make_async_copy(index_hbm, index_ref, sems.at[3]),
    ]
    for copy in copies:
        copy.start()
    copies[0].wait()
    centred = (held[...] - SHIFT) * ROOT
    out_ref[0:rows, :] = centred
    front, parts = packed_parts(points)
    last = 3 * (points // 4)
    packed_ref[0:rows, front] = centred[:, :last]
    for part, columns in enumerate(parts):
        packed_ref[rows:rows + 2, columns] = out_ref[2 * part:2 * part + 2, last:]
    out_ref[rows:rows + 1, :] = -0.5 * jnp.sum(centred * centred, axis=0, keepdims=True)
    out_ref[rows + 1:rows + 2, :] = jnp.ones((1, points), F32)
    for copy in copies[1:]:
        copy.wait()


def extend(coords, right_sides, skel_index):
    rows, points = coords.shape
    return pl.pallas_call(
        extend_kernel,
        out_shape=(
            pltpu.VMEM((16, points), F32),
            pltpu.VMEM((8, points + 3 * (points // 4)), F32),
            pltpu.VMEM(skel_index.shape, jnp.int32),
        ),
        in_specs=[HBM_SPEC] * 3,
        out_specs=(VMEM_SPEC,) * 3,
        scratch_shapes=[pltpu.VMEM((rows, points), F32), pltpu.SemaphoreType.DMA((4,))],
        compiler_params=pltpu.CompilerParams(vmem_limit_bytes=58 * 2**20),
        name="extend",
    )(coords, right_sides, skel_index)


def first_kernel(leaf, x_ref, proj_ref, index_ref, node_ref, self_ref, held, sources, weights, targets, sems):
    chunks = held.shape[0]
    chunk, rank = held.shape[1:]
    points = x_ref.shape[1]
    copies = [
        pltpu.make_async_copy(proj_ref.at[pl.ds(at * chunk, chunk)], held.at[at], sems.at[at]) for at in range(chunks)
    ]
    for copy in copies:
        copy.start()
    for half in range(rank // LANES):
        lanes = slice(half * LANES, (half + 1) * LANES)
        pieces = [x_ref[0:8, at * LANES:(at + 1) * LANES] for at in range(points // LANES)]
        columns = pick_columns(pieces, index_ref[:, lanes])
        for copy in range(node_ref.shape[0]):
            node_ref[copy, 0:8, lanes] = columns
    wide = 8 * leaf

    def prepare(at, _):
        columns = pl.ds(pl.multiple_of(at * wide, wide), wide)
        sources[:, columns] = source_form(x_ref[0:8, columns])
        twice = pl.ds(pl.multiple_of(at * 2 * wide, wide), 2 * wide)
        weights[:, twice] = repeat_blocks(weight_form(x_ref[8:16, columns]))
        targets[:, columns] = target_form(x_ref[0:8, columns])
        return 0

    def turn(at, _):
        for part in range(LEAVES_SELF):
            columns = pl.ds(pl.multiple_of((at * LEAVES_SELF + part) * leaf, leaf), leaf)
            twice = pl.ds(pl.multiple_of((at * LEAVES_SELF + part) * 2 * leaf, leaf), 2 * leaf)
            self_ref[:, columns] = fold(kernel_term(sources[:, columns].T, targets[:, columns], weights[:, twice]))
        return 0

    lax.fori_loop(0, points // wide, prepare, 0)
    lax.fori_loop(0, points // (leaf * LEAVES_SELF), turn, 0)
    total = jnp.zeros((8, rank), F32)
    for at in range(chunks):
        x_high, x_low = two_pieces(x_ref[8:16, at * chunk:(at + 1) * chunk])
        left = jnp.concatenate([x_high, x_low], axis=0).astype(BF16)
        copies[at].wait()
        p_high, p_low = two_pieces(held[at])
        both = jnp.dot(left, p_high.astype(BF16), preferred_element_type=F32)
        part = jnp.dot(left, p_low.astype(BF16), preferred_element_type=F32)
        total += both[:8] + both[8:] + part[:8]
    for copy in range(node_ref.shape[0]):
        node_ref[copy, 8:16, :] = total


def first_step(copies, leaf, extended, projection, skel_index):
    points, rank = projection.shape
    chunks = 8
    return pl.pallas_call(
        functools.partial(first_kernel, leaf),
        out_shape=(
            jax.ShapeDtypeStruct((copies, 16, rank), F32),
            jax.ShapeDtypeStruct((8, points), F32),
        ),
        in_specs=[VMEM_SPEC, HBM_SPEC, VMEM_SPEC],
        out_specs=(VMEM_SPEC, VMEM_SPEC),
        scratch_shapes=[
            pltpu.VMEM((chunks, points // chunks, rank), F32),
            pltpu.VMEM((48, points), BF16),
            pltpu.VMEM((16, 2 * points), BF16),
            pltpu.VMEM((48, points), BF16),
            pltpu.SemaphoreType.DMA((chunks,)),
        ],
        compiler_params=pltpu.CompilerParams(vmem_limit_bytes=50 * 2**20),
        name="first_step",
    )(extended, projection, skel_index)


def climb(source, first, count, selection, rows, transfer, target, offset):
    rank = transfer[0].shape[1]
    t_high, t_low = transfer
    joined = jnp.concatenate(
        [
            jnp.concatenate([source[first + 2 * m + side, 8:16, :] for m in range(count)], axis=0)
            for side in range(2)
        ],
        axis=1,
    )
    high, low = two_pieces(joined)
    left = jnp.concatenate([high, low], axis=0).astype(BF16)
    both = jnp.dot(left, t_high, preferred_element_type=F32)
    part = jnp.dot(left, t_low, preferred_element_type=F32)
    moved = both[:8 * count] + both[8 * count:] + part[:8 * count]
    for m in range(count):
        target[offset + m, 8:16, :] = moved[m * 8:(m + 1) * 8, :]
        pieces = [
            source[first + 2 * m + side, 0:8, at * LANES:(at + 1) * LANES]
            for side in range(2)
            for at in range(rank // LANES)
        ]
        picked = selection[pl.ds(rows + m, 1), :]
        for half in range(rank // LANES):
            lanes = slice(half * LANES, (half + 1) * LANES)
            target[offset + m, 0:8, lanes] = pick_columns(pieces, picked[:, lanes])


def split_transfer(transfer_ref):
    t_high, t_low = two_pieces(transfer_ref[...])
    return t_high.astype(BF16), t_low.astype(BF16)


def near_kernel(near_ref, count_ref, self_ref, chip_ref, own_ref, other_ref, out_ref, sources, weights, targets, unpacked):
    leaves, slots = near_ref.shape
    points = own_ref.shape[1]
    leaf = points // leaves
    own_index = lax.axis_index("leaf")
    even = own_index % 2 == 0
    first_leaf = own_index * leaves
    wide = 8 * leaf

    front, parts = packed_parts(points)
    last = 3 * (points // 4)
    unpacked[0:6, 0:last] = other_ref[0:6, front]
    for part, columns in enumerate(parts):
        unpacked[2 * part:2 * part + 2, last:] = other_ref[6:8, columns]
    add_norm(unpacked)

    def prepare(at, _):
        columns = pl.ds(pl.multiple_of(at * wide, wide), wide)
        for part, (coords, values) in enumerate(
            ((chip_ref, chip_ref.at[pl.ds(8, 8)]), (own_ref, own_ref.at[pl.ds(8, 8)]), (unpacked, other_ref))
        ):
            window = pl.ds(pl.multiple_of(part * points + at * wide, wide), wide)
            sources[:, window] = source_form(coords[0:8, columns])
            twice = pl.ds(pl.multiple_of(2 * (part * points + at * wide), wide), 2 * wide)
            weights[:, twice] = repeat_blocks(weight_form(values[0:8, columns]))
        targets[:, columns] = target_form(own_ref[0:8, columns])
        return 0

    lax.fori_loop(0, points // wide, prepare, 0)

    def window_place(offset):
        below, above = offset < 0, offset >= leaves
        left = jnp.where(even, 2, 0)
        part = jnp.where(below, left, jnp.where(above, 2 - left, 1))
        local = jnp.where(below, offset + leaves, jnp.where(above, offset - leaves, offset))
        return part * leaves + jnp.clip(local, 0, leaves - 1)

    def one_leaf(at, live_slots):
        columns = pl.ds(pl.multiple_of(at * leaf, leaf), leaf)
        target = targets[:, columns]
        held, pieces = [], []
        for slot in range(1, live_slots):
            place = window_place(near_ref[at, slot] - first_leaf)
            window = pl.ds(pl.multiple_of(place * leaf, leaf), leaf)
            weight = weights[:, pl.ds(pl.multiple_of(place * 2 * leaf, leaf), 2 * leaf)]
            held.append(jnp.where(slot < count_ref[at], weight, jnp.zeros_like(weight)))
            pieces += kernel_pieces(sources[:, window].T, target, LANES, LANES)
        out_ref[:, columns] = self_ref[:, columns] + weigh(held, pieces)

    def turn(at, _):
        most = count_ref[NEAR_TURN * at]
        for leaf_at in range(1, NEAR_TURN):
            most = jnp.maximum(most, count_ref[NEAR_TURN * at + leaf_at])
        heavy = most > slots // 2

        @pl.when(heavy)
        def _():
            for leaf_at in range(NEAR_TURN):
                one_leaf(NEAR_TURN * at + leaf_at, slots)

        @pl.when(jnp.logical_not(heavy))
        def _():
            for leaf_at in range(NEAR_TURN):
                one_leaf(NEAR_TURN * at + leaf_at, slots // 2)

        return 0

    lax.fori_loop(0, leaves // NEAR_TURN, turn, 0)


def near_term(near_leaf, near_count, own_part, chip, own, other):
    leaves, slots = near_leaf.shape
    points = own.shape[1]
    entries = leaves * slots * (points // leaves) ** 2
    return pl.pallas_call(
        near_kernel,
        out_shape=jax.ShapeDtypeStruct((8, points), F32),
        in_specs=[SMEM_SPEC] * 2 + [VMEM_SPEC] * 4,
        out_specs=VMEM_SPEC,
        scratch_shapes=[
            pltpu.VMEM((48, 3 * points), BF16),
            pltpu.VMEM((16, 6 * points), BF16),
            pltpu.VMEM((48, points), BF16),
            pltpu.VMEM((8, points), F32),
        ],
        cost_estimate=pl.CostEstimate(flops=1000 * entries, bytes_accessed=4 * 64 * points, transcendentals=entries),
        compiler_params=pltpu.CompilerParams(vmem_limit_bytes=32 * 2**20),
        name="near_term",
    )(near_leaf, near_count, own_part, chip, own, other)


def far_kernel(scale, tile, own_ref, near_ref, gathered_ref, selection_ref, transfer_ref, out_ref, nodes, sources, weights):
    devices = gathered_ref.shape[0]
    levels = devices.bit_length() - 1
    own_index = lax.axis_index("leaf")
    transfer = split_transfer(transfer_ref)
    rank = transfer_ref.shape[1]
    held, first = gathered_ref, 0
    for level in range(levels):
        node = held[first + ((own_index >> level) ^ 1)]
        form = source_form(node[0:8])
        form = jnp.concatenate([form, jnp.zeros((LANES - 48, rank), BF16)], axis=0)
        sources[level * rank:(level + 1) * rank] = form.T
        form = weight_form(node[8:16])
        weights[level] = jnp.concatenate([form, form], axis=1)
        if level < levels - 1:
            rows = devices - (devices >> level)
            climb(held, first, devices >> (level + 1), selection_ref, rows, transfer, nodes, rows)
            held, first = nodes, rows

    def turn(at, _):
        for part in range(FAR_TURN):
            columns = pl.ds(pl.multiple_of((at * FAR_TURN + part) * tile, tile), tile)
            target = target_form(own_ref[0:8, columns])
            target = jnp.concatenate([target, jnp.zeros((LANES - 48, tile), BF16)], axis=0)
            pieces = []
            for level in range(0, levels, 2):
                pair = sources[level * rank:min(level + 2, levels) * rank]
                exponent = jnp.dot(pair, target, preferred_element_type=F32)
                for first in range(0, pair.shape[0], rank):
                    pieces += split_block(exponent[first:first + rank])
            total = weigh([weights[level] for level in range(levels)], pieces)
            out_ref[:, columns] = (total + near_ref[:, columns]) * scale
        return 0

    lax.fori_loop(0, own_ref.shape[1] // (tile * FAR_TURN), turn, 0)


def far_term(scale, tile, own, near, gathered, selection, transfer):
    devices, _, rank = gathered.shape
    levels = devices.bit_length() - 1
    return pl.pallas_call(
        functools.partial(far_kernel, scale, tile),
        out_shape=jax.ShapeDtypeStruct((8, own.shape[1]), F32),
        in_specs=[VMEM_SPEC] * 5,
        out_specs=VMEM_SPEC,
        scratch_shapes=[
            pltpu.VMEM((devices - 2, 16, rank), F32),
            pltpu.VMEM((levels * rank, LANES), BF16),
            pltpu.VMEM((levels, 16, 2 * rank), BF16),
        ],
        compiler_params=pltpu.CompilerParams(vmem_limit_bytes=32 * 2**20),
        name="far_term",
    )(own, near, gathered, selection, transfer)


def body(coords, right_sides, projection, skel_index, selection, transfer, near_leaf, near_count):
    devices = lax.axis_size("leaf")
    leaves, slots = near_leaf.shape
    leaf = coords.shape[1] // leaves
    scale = 1.0 / (slots * leaf) ** 0.5
    extended, packed, skel_index = extend(coords, right_sides, skel_index)
    chip = swap(extended, "leaf", 0)
    other = swap(packed, "leaf", 1)
    node, own_part = first_step(devices, leaf, extended, projection, skel_index)
    gathered = lax.all_to_all(node, "leaf", 0, 0, tiled=True)
    near = near_term(near_leaf, near_count, own_part, chip, extended, other)
    return far_term(scale, leaf, extended, near, gathered, selection, transfer)


def solution(mesh):
    return jax.shard_map(
        body,
        mesh=mesh,
        in_specs=(
            P(None, "leaf"),
            P(None, "leaf"),
            P("leaf", None),
            P("leaf", None),
            P(),
            P(),
            P("leaf", None),
            P("leaf"),
        ),
        out_specs=P(None, "leaf"),
        check_vma=False,
    )
```

```python
import functools
import math

import jax
import jax.numpy as jnp
from jax import lax
from jax.experimental import pallas as pl
from jax.experimental.pallas import tpu as pltpu
from jax.sharding import PartitionSpec as P

F32 = jnp.float32
BF16 = jnp.bfloat16
LANES = 128
SHIFT = 2.0
NEAR_TURN = 16
FAR_TURN = 32
LEAVES_SELF = 16
ROOT = math.sqrt(math.log2(math.e))
SMEM_SPEC = pl.BlockSpec(memory_space=pltpu.SMEM)
HBM_SPEC = pl.BlockSpec(memory_space=pltpu.HBM)
VMEM_SPEC = pl.BlockSpec(memory_space=pltpu.VMEM)


def swap(value, axis, first):
    count = lax.axis_size(axis)
    pairs = []
    for left in range(first, count - 1, 2):
        pairs += [(left, left + 1), (left + 1, left)]
    return lax.ppermute(value, axis, pairs)


def two_pieces(value):
    high = value.astype(BF16).astype(F32)
    return high, value - high


def three_pieces(value):
    high, rest = two_pieces(value)
    middle, low = two_pieces(rest)
    return high, middle, low


def source_form(extended):
    high, middle, low = three_pieces(extended)
    return jnp.concatenate([high, high, high, middle, middle, low], axis=0).astype(BF16)


def target_form(extended):
    row = lax.broadcasted_iota(jnp.int32, extended.shape, 0)
    below = pltpu.roll(extended, 1, 0)
    swapped = jnp.where(row == 6, 1.0, jnp.where(row == 7, below, extended))
    high, middle, low = three_pieces(swapped)
    return jnp.concatenate([high, middle, low, high, middle, high], axis=0).astype(BF16)


def weight_form(values):
    high, low = two_pieces(values)
    return jnp.concatenate([high, low], axis=0).astype(BF16)


def pick_columns(pieces, index):
    index = jnp.broadcast_to(index, (8, LANES))
    low = index & (LANES - 1)
    high = index >> 7
    result = jnp.take_along_axis(pieces[0], low, axis=1)
    for at in range(1, len(pieces)):
        result = jnp.where(high == at, jnp.take_along_axis(pieces[at], low, axis=1), result)
    return result


def split_block(exponent):
    kernel = jnp.exp2(jnp.minimum(exponent, 0.0))
    high = kernel.astype(BF16)
    return high, (kernel - high.astype(F32)).astype(BF16)


def repeat_blocks(weight):
    pieces = []
    for first in range(0, weight.shape[1], LANES):
        pieces += [weight[:, first:first + LANES]] * 2
    return jnp.concatenate(pieces, axis=1)


def kernel_term(source, target, weight):
    total = None
    for first in range(0, source.shape[0], LANES):
        high, low = split_block(jnp.dot(source[first:first + LANES], target, preferred_element_type=F32))
        both = jnp.concatenate([high, low], axis=0)
        term = jnp.dot(weight[:, 2 * first:2 * (first + LANES)], both, preferred_element_type=F32)
        total = term if total is None else total + term
    return total


def kernel_pieces(source, target, rows, chunk):
    pieces = []
    for first in range(0, source.shape[0], rows):
        split = [
            split_block(jnp.dot(source[at:at + chunk], target, preferred_element_type=F32))
            for at in range(first, first + rows, chunk)
        ]
        pieces += [high for high, _ in split] + [low for _, low in split]
    return pieces


def weigh(weights, pieces):
    weights = jnp.concatenate(weights, axis=1)
    return fold(jnp.dot(weights, jnp.concatenate(pieces, axis=0), preferred_element_type=F32))


def fold(pieces):
    return pieces[:8] + pieces[8:]


def add_norm(ref):
    centred = ref[0:6, :]
    ref[6:7, :] = -0.5 * jnp.sum(centred * centred, axis=0, keepdims=True)
    ref[7:8, :] = jnp.ones((1, centred.shape[1]), F32)


def packed_parts(points):
    quarter = points // 4
    return slice(points, points + 3 * quarter), [
        slice(points + part * quarter, points + (part + 1) * quarter) for part in range(3)
    ]


def extend_kernel(coords_ref, right_ref, index_hbm, out_ref, packed_ref, index_ref, held, sems):
    rows, points = held.shape
    copies = [
        pltpu.make_async_copy(coords_ref, held, sems.at[0]),
        pltpu.make_async_copy(right_ref, out_ref.at[pl.ds(8, 8)], sems.at[1]),
        pltpu.make_async_copy(right_ref, packed_ref.at[:, pl.ds(0, points)], sems.at[2]),
        pltpu.make_async_copy(index_hbm, index_ref, sems.at[3]),
    ]
    for copy in copies:
        copy.start()
    copies[0].wait()
    centred = (held[...] - SHIFT) * ROOT
    out_ref[0:rows, :] = centred
    front, parts = packed_parts(points)
    last = 3 * (points // 4)
    packed_ref[0:rows, front] = centred[:, :last]
    for part, columns in enumerate(parts):
        packed_ref[rows:rows + 2, columns] = out_ref[2 * part:2 * part + 2, last:]
    out_ref[rows:rows + 1, :] = -0.5 * jnp.sum(centred * centred, axis=0, keepdims=True)
    out_ref[rows + 1:rows + 2, :] = jnp.ones((1, points), F32)
    for copy in copies[1:]:
        copy.wait()


def extend(coords, right_sides, skel_index):
    rows, points = coords.shape
    return pl.pallas_call(
        extend_kernel,
        out_shape=(
            pltpu.VMEM((16, points), F32),
            pltpu.VMEM((8, points + 3 * (points // 4)), F32),
            pltpu.VMEM(skel_index.shape, jnp.int32),
        ),
        in_specs=[HBM_SPEC] * 3,
        out_specs=(VMEM_SPEC,) * 3,
        scratch_shapes=[pltpu.VMEM((rows, points), F32), pltpu.SemaphoreType.DMA((4,))],
        compiler_params=pltpu.CompilerParams(vmem_limit_bytes=58 * 2**20),
        name="extend",
    )(coords, right_sides, skel_index)


def first_kernel(leaf, x_ref, proj_ref, index_ref, node_ref, self_ref, held, sources, weights, targets, sems):
    chunks = held.shape[0]
    chunk, rank = held.shape[1:]
    points = x_ref.shape[1]
    copies = [
        pltpu.make_async_copy(proj_ref.at[pl.ds(at * chunk, chunk)], held.at[at], sems.at[at]) for at in range(chunks)
    ]
    for copy in copies:
        copy.start()
    for half in range(rank // LANES):
        lanes = slice(half * LANES, (half + 1) * LANES)
        pieces = [x_ref[0:8, at * LANES:(at + 1) * LANES] for at in range(points // LANES)]
        columns = pick_columns(pieces, index_ref[:, lanes])
        for copy in range(node_ref.shape[0]):
            node_ref[copy, 0:8, lanes] = columns
    wide = 8 * leaf

    def prepare(at, _):
        columns = pl.ds(pl.multiple_of(at * wide, wide), wide)
        sources[:, columns] = source_form(x_ref[0:8, columns])
        twice = pl.ds(pl.multiple_of(at * 2 * wide, wide), 2 * wide)
        weights[:, twice] = repeat_blocks(weight_form(x_ref[8:16, columns]))
        targets[:, columns] = target_form(x_ref[0:8, columns])
        return 0

    def turn(at, _):
        for part in range(LEAVES_SELF):
            columns = pl.ds(pl.multiple_of((at * LEAVES_SELF + part) * leaf, leaf), leaf)
            twice = pl.ds(pl.multiple_of((at * LEAVES_SELF + part) * 2 * leaf, leaf), 2 * leaf)
            self_ref[:, columns] = fold(kernel_term(sources[:, columns].T, targets[:, columns], weights[:, twice]))
        return 0

    lax.fori_loop(0, points // wide, prepare, 0)
    lax.fori_loop(0, points // (leaf * LEAVES_SELF), turn, 0)
    total = jnp.zeros((8, rank), F32)
    for at in range(chunks):
        x_high, x_low = two_pieces(x_ref[8:16, at * chunk:(at + 1) * chunk])
        left = jnp.concatenate([x_high, x_low], axis=0).astype(BF16)
        copies[at].wait()
        p_high, p_low = two_pieces(held[at])
        both = jnp.dot(left, p_high.astype(BF16), preferred_element_type=F32)
        part = jnp.dot(left, p_low.astype(BF16), preferred_element_type=F32)
        total += both[:8] + both[8:] + part[:8]
    for copy in range(node_ref.shape[0]):
        node_ref[copy, 8:16, :] = total


def first_step(copies, leaf, extended, projection, skel_index):
    points, rank = projection.shape
    chunks = 8
    return pl.pallas_call(
        functools.partial(first_kernel, leaf),
        out_shape=(
            jax.ShapeDtypeStruct((copies, 16, rank), F32),
            jax.ShapeDtypeStruct((8, points), F32),
        ),
        in_specs=[VMEM_SPEC, HBM_SPEC, VMEM_SPEC],
        out_specs=(VMEM_SPEC, VMEM_SPEC),
        scratch_shapes=[
            pltpu.VMEM((chunks, points // chunks, rank), F32),
            pltpu.VMEM((48, points), BF16),
            pltpu.VMEM((16, 2 * points), BF16),
            pltpu.VMEM((48, points), BF16),
            pltpu.SemaphoreType.DMA((chunks,)),
        ],
        compiler_params=pltpu.CompilerParams(vmem_limit_bytes=50 * 2**20),
        name="first_step",
    )(extended, projection, skel_index)


def climb(source, first, count, selection, rows, transfer, target, offset):
    rank = transfer[0].shape[1]
    t_high, t_low = transfer
    joined = jnp.concatenate(
        [
            jnp.concatenate([source[first + 2 * m + side, 8:16, :] for m in range(count)], axis=0)
            for side in range(2)
        ],
        axis=1,
    )
    high, low = two_pieces(joined)
    left = jnp.concatenate([high, low], axis=0).astype(BF16)
    both = jnp.dot(left, t_high, preferred_element_type=F32)
    part = jnp.dot(left, t_low, preferred_element_type=F32)
    moved = both[:8 * count] + both[8 * count:] + part[:8 * count]
    for m in range(count):
        target[offset + m, 8:16, :] = moved[m * 8:(m + 1) * 8, :]
        pieces = [
            source[first + 2 * m + side, 0:8, at * LANES:(at + 1) * LANES]
            for side in range(2)
            for at in range(rank // LANES)
        ]
        picked = selection[pl.ds(rows + m, 1), :]
        for half in range(rank // LANES):
            lanes = slice(half * LANES, (half + 1) * LANES)
            target[offset + m, 0:8, lanes] = pick_columns(pieces, picked[:, lanes])


def split_transfer(transfer_ref):
    t_high, t_low = two_pieces(transfer_ref[...])
    return t_high.astype(BF16), t_low.astype(BF16)


def near_kernel(near_ref, count_ref, self_ref, chip_ref, own_ref, other_ref, out_ref, sources, weights, targets, unpacked):
    leaves, slots = near_ref.shape
    points = own_ref.shape[1]
    leaf = points // leaves
    own_index = lax.axis_index("leaf")
    even = own_index % 2 == 0
    first_leaf = own_index * leaves
    wide = 8 * leaf

    front, parts = packed_parts(points)
    last = 3 * (points // 4)
    unpacked[0:6, 0:last] = other_ref[0:6, front]
    for part, columns in enumerate(parts):
        unpacked[2 * part:2 * part + 2, last:] = other_ref[6:8, columns]
    add_norm(unpacked)

    def prepare(at, _):
        columns = pl.ds(pl.multiple_of(at * wide, wide), wide)
        for part, (coords, values) in enumerate(
            ((chip_ref, chip_ref.at[pl.ds(8, 8)]), (own_ref, own_ref.at[pl.ds(8, 8)]), (unpacked, other_ref))
        ):
            window = pl.ds(pl.multiple_of(part * points + at * wide, wide), wide)
            sources[:, window] = source_form(coords[0:8, columns])
            twice = pl.ds(pl.multiple_of(2 * (part * points + at * wide), wide), 2 * wide)
            weights[:, twice] = repeat_blocks(weight_form(values[0:8, columns]))
        targets[:, columns] = target_form(own_ref[0:8, columns])
        return 0

    lax.fori_loop(0, points // wide, prepare, 0)

    def window_place(offset):
        below, above = offset < 0, offset >= leaves
        left = jnp.where(even, 2, 0)
        part = jnp.where(below, left, jnp.where(above, 2 - left, 1))
        local = jnp.where(below, offset + leaves, jnp.where(above, offset - leaves, offset))
        return part * leaves + jnp.clip(local, 0, leaves - 1)

    def one_leaf(at, live_slots):
        columns = pl.ds(pl.multiple_of(at * leaf, leaf), leaf)
        target = targets[:, columns]
        held, pieces = [], []
        for slot in range(1, live_slots):
            place = window_place(near_ref[at, slot] - first_leaf)
            window = pl.ds(pl.multiple_of(place * leaf, leaf), leaf)
            weight = weights[:, pl.ds(pl.multiple_of(place * 2 * leaf, leaf), 2 * leaf)]
            held.append(jnp.where(slot < count_ref[at], weight, jnp.zeros_like(weight)))
            pieces += kernel_pieces(sources[:, window].T, target, LANES, LANES)
        out_ref[:, columns] = self_ref[:, columns] + weigh(held, pieces)

    def turn(at, _):
        most = count_ref[NEAR_TURN * at]
        for leaf_at in range(1, NEAR_TURN):
            most = jnp.maximum(most, count_ref[NEAR_TURN * at + leaf_at])
        heavy = most > slots // 2

        @pl.when(heavy)
        def _():
            for leaf_at in range(NEAR_TURN):
                one_leaf(NEAR_TURN * at + leaf_at, slots)

        @pl.when(jnp.logical_not(heavy))
        def _():
            for leaf_at in range(NEAR_TURN):
                one_leaf(NEAR_TURN * at + leaf_at, slots // 2)

        return 0

    lax.fori_loop(0, leaves // NEAR_TURN, turn, 0)


def near_term(near_leaf, near_count, own_part, chip, own, other):
    leaves, slots = near_leaf.shape
    points = own.shape[1]
    entries = leaves * slots * (points // leaves) ** 2
    return pl.pallas_call(
        near_kernel,
        out_shape=jax.ShapeDtypeStruct((8, points), F32),
        in_specs=[SMEM_SPEC] * 2 + [VMEM_SPEC] * 4,
        out_specs=VMEM_SPEC,
        scratch_shapes=[
            pltpu.VMEM((48, 3 * points), BF16),
            pltpu.VMEM((16, 6 * points), BF16),
            pltpu.VMEM((48, points), BF16),
            pltpu.VMEM((8, points), F32),
        ],
        cost_estimate=pl.CostEstimate(flops=1000 * entries, bytes_accessed=4 * 64 * points, transcendentals=entries),
        compiler_params=pltpu.CompilerParams(vmem_limit_bytes=32 * 2**20),
        name="near_term",
    )(near_leaf, near_count, own_part, chip, own, other)


def far_kernel(scale, tile, own_ref, near_ref, gathered_ref, selection_ref, transfer_ref, out_ref, nodes, sources, weights):
    devices = gathered_ref.shape[0]
    levels = devices.bit_length() - 1
    own_index = lax.axis_index("leaf")
    transfer = split_transfer(transfer_ref)
    rank = transfer_ref.shape[1]
    held, first = gathered_ref, 0
    for level in range(levels):
        node = held[first + ((own_index >> level) ^ 1)]
        form = source_form(node[0:8])
        sources[level] = jnp.concatenate([form, jnp.zeros((LANES - 48, rank), BF16)], axis=0).T
        form = weight_form(node[8:16])
        weights[level] = jnp.concatenate([form, form], axis=1)
        if level < levels - 1:
            rows = devices - (devices >> level)
            climb(held, first, devices >> (level + 1), selection_ref, rows, transfer, nodes, rows)
            held, first = nodes, rows

    def turn(at, _):
        for part in range(FAR_TURN):
            columns = pl.ds(pl.multiple_of((at * FAR_TURN + part) * tile, tile), tile)
            target = target_form(own_ref[0:8, columns])
            target = jnp.concatenate([target, jnp.zeros((LANES - 48, tile), BF16)], axis=0)
            pieces = []
            for level in range(levels):
                pieces += kernel_pieces(sources[level], target, rank, rank)
            total = weigh([weights[level] for level in range(levels)], pieces)
            out_ref[:, columns] = (total + near_ref[:, columns]) * scale
        return 0

    lax.fori_loop(0, own_ref.shape[1] // (tile * FAR_TURN), turn, 0)


def far_term(scale, tile, own, near, gathered, selection, transfer):
    devices, _, rank = gathered.shape
    levels = devices.bit_length() - 1
    return pl.pallas_call(
        functools.partial(far_kernel, scale, tile),
        out_shape=jax.ShapeDtypeStruct((8, own.shape[1]), F32),
        in_specs=[VMEM_SPEC] * 5,
        out_specs=VMEM_SPEC,
        scratch_shapes=[
            pltpu.VMEM((devices - 2, 16, rank), F32),
            pltpu.VMEM((levels, rank, LANES), BF16),
            pltpu.VMEM((levels, 16, 2 * rank), BF16),
        ],
        compiler_params=pltpu.CompilerParams(vmem_limit_bytes=32 * 2**20),
        name="far_term",
    )(own, near, gathered, selection, transfer)


def body(coords, right_sides, projection, skel_index, selection, transfer, near_leaf, near_count):
    devices = lax.axis_size("leaf")
    leaves, slots = near_leaf.shape
    leaf = coords.shape[1] // leaves
    scale = 1.0 / (slots * leaf) ** 0.5
    extended, packed, skel_index = extend(coords, right_sides, skel_index)
    chip = swap(extended, "leaf", 0)
    other = swap(packed, "leaf", 1)
    node, own_part = first_step(devices, leaf, extended, projection, skel_index)
    gathered = lax.all_to_all(node, "leaf", 0, 0, tiled=True)
    near = near_term(near_leaf, near_count, own_part, chip, extended, other)
    return far_term(scale, leaf, extended, near, gathered, selection, transfer)


def solution(mesh):
    return jax.shard_map(
        body,
        mesh=mesh,
        in_specs=(
            P(None, "leaf"),
            P(None, "leaf"),
            P("leaf", None),
            P("leaf", None),
            P(),
            P(),
            P("leaf", None),
            P("leaf"),
        ),
        out_specs=P(None, "leaf"),
        check_vma=False,
    )
```

```python
import functools
import math

import jax
import jax.numpy as jnp
from jax import lax
from jax.experimental import pallas as pl
from jax.experimental.pallas import tpu as pltpu
from jax.sharding import PartitionSpec as P

F32 = jnp.float32
BF16 = jnp.bfloat16
LANES = 128
SHIFT = 2.0
NEAR_TURN = 16
FAR_TURN = 32
LEAVES_SELF = 16
ROOT = math.sqrt(math.log2(math.e))
SMEM_SPEC = pl.BlockSpec(memory_space=pltpu.SMEM)
HBM_SPEC = pl.BlockSpec(memory_space=pltpu.HBM)
VMEM_SPEC = pl.BlockSpec(memory_space=pltpu.VMEM)


def swap(value, axis, first):
    count = lax.axis_size(axis)
    pairs = []
    for left in range(first, count - 1, 2):
        pairs += [(left, left + 1), (left + 1, left)]
    return lax.ppermute(value, axis, pairs)


def two_pieces(value):
    high = value.astype(BF16).astype(F32)
    return high, value - high


def three_pieces(value):
    high, rest = two_pieces(value)
    middle, low = two_pieces(rest)
    return high, middle, low


def source_form(extended):
    high, middle, low = three_pieces(extended)
    return jnp.concatenate([high, high, high, middle, middle, low], axis=0).astype(BF16)


def target_form(extended):
    row = lax.broadcasted_iota(jnp.int32, extended.shape, 0)
    below = pltpu.roll(extended, 1, 0)
    swapped = jnp.where(row == 6, 1.0, jnp.where(row == 7, below, extended))
    high, middle, low = three_pieces(swapped)
    return jnp.concatenate([high, middle, low, high, middle, high], axis=0).astype(BF16)


def weight_form(values):
    high, low = two_pieces(values)
    return jnp.concatenate([high, low], axis=0).astype(BF16)


def pick_columns(pieces, index):
    index = jnp.broadcast_to(index, (8, LANES))
    low = index & (LANES - 1)
    high = index >> 7
    result = jnp.take_along_axis(pieces[0], low, axis=1)
    for at in range(1, len(pieces)):
        result = jnp.where(high == at, jnp.take_along_axis(pieces[at], low, axis=1), result)
    return result


def split_block(exponent):
    kernel = jnp.exp2(jnp.minimum(exponent, 0.0))
    high = kernel.astype(BF16)
    return high, (kernel - high.astype(F32)).astype(BF16)


def repeat_blocks(weight):
    pieces = []
    for first in range(0, weight.shape[1], LANES):
        pieces += [weight[:, first:first + LANES]] * 2
    return jnp.concatenate(pieces, axis=1)


def kernel_term(source, target, weight):
    total = None
    for first in range(0, source.shape[0], LANES):
        high, low = split_block(jnp.dot(source[first:first + LANES], target, preferred_element_type=F32))
        both = jnp.concatenate([high, low], axis=0)
        term = jnp.dot(weight[:, 2 * first:2 * (first + LANES)], both, preferred_element_type=F32)
        total = term if total is None else total + term
    return total


def kernel_pieces(source, target, rows, chunk):
    pieces = []
    for first in range(0, source.shape[0], rows):
        split = [
            split_block(jnp.dot(source[at:at + chunk], target, preferred_element_type=F32))
            for at in range(first, first + rows, chunk)
        ]
        pieces += [high for high, _ in split] + [low for _, low in split]
    return pieces


def weigh(weights, pieces):
    weights = jnp.concatenate(weights, axis=1)
    return fold(jnp.dot(weights, jnp.concatenate(pieces, axis=0), preferred_element_type=F32))


def fold(pieces):
    return pieces[:8] + pieces[8:]


def add_norm(ref):
    centred = ref[0:6, :]
    ref[6:7, :] = -0.5 * jnp.sum(centred * centred, axis=0, keepdims=True)
    ref[7:8, :] = jnp.ones((1, centred.shape[1]), F32)


def packed_parts(points):
    quarter = points // 4
    return slice(points, points + 3 * quarter), [
        slice(points + part * quarter, points + (part + 1) * quarter) for part in range(3)
    ]


def extend_kernel(coords_ref, right_ref, index_hbm, out_ref, packed_ref, index_ref, held, sems):
    rows, points = held.shape
    copies = [
        pltpu.make_async_copy(coords_ref, held, sems.at[0]),
        pltpu.make_async_copy(right_ref, out_ref.at[pl.ds(8, 8)], sems.at[1]),
        pltpu.make_async_copy(right_ref, packed_ref.at[:, pl.ds(0, points)], sems.at[2]),
        pltpu.make_async_copy(index_hbm, index_ref, sems.at[3]),
    ]
    for copy in copies:
        copy.start()
    copies[0].wait()
    centred = (held[...] - SHIFT) * ROOT
    out_ref[0:rows, :] = centred
    front, parts = packed_parts(points)
    last = 3 * (points // 4)
    packed_ref[0:rows, front] = centred[:, :last]
    for part, columns in enumerate(parts):
        packed_ref[rows:rows + 2, columns] = out_ref[2 * part:2 * part + 2, last:]
    out_ref[rows:rows + 1, :] = -0.5 * jnp.sum(centred * centred, axis=0, keepdims=True)
    out_ref[rows + 1:rows + 2, :] = jnp.ones((1, points), F32)
    for copy in copies[1:]:
        copy.wait()


def extend(coords, right_sides, skel_index):
    rows, points = coords.shape
    return pl.pallas_call(
        extend_kernel,
        out_shape=(
            pltpu.VMEM((16, points), F32),
            pltpu.VMEM((8, points + 3 * (points // 4)), F32),
            pltpu.VMEM(skel_index.shape, jnp.int32),
        ),
        in_specs=[HBM_SPEC] * 3,
        out_specs=(VMEM_SPEC,) * 3,
        scratch_shapes=[pltpu.VMEM((rows, points), F32), pltpu.SemaphoreType.DMA((4,))],
        compiler_params=pltpu.CompilerParams(vmem_limit_bytes=58 * 2**20),
        name="extend",
    )(coords, right_sides, skel_index)


def first_kernel(leaf, x_ref, proj_ref, index_ref, node_ref, self_ref, held, sources, weights, targets, sems):
    chunks = held.shape[0]
    chunk, rank = held.shape[1:]
    points = x_ref.shape[1]
    copies = [
        pltpu.make_async_copy(proj_ref.at[pl.ds(at * chunk, chunk)], held.at[at], sems.at[at]) for at in range(chunks)
    ]
    for copy in copies:
        copy.start()
    for half in range(rank // LANES):
        lanes = slice(half * LANES, (half + 1) * LANES)
        pieces = [x_ref[0:8, at * LANES:(at + 1) * LANES] for at in range(points // LANES)]
        columns = pick_columns(pieces, index_ref[:, lanes])
        for copy in range(node_ref.shape[0]):
            node_ref[copy, 0:8, lanes] = columns
    wide = 8 * leaf

    def prepare(at, _):
        columns = pl.ds(pl.multiple_of(at * wide, wide), wide)
        sources[:, columns] = source_form(x_ref[0:8, columns])
        twice = pl.ds(pl.multiple_of(at * 2 * wide, wide), 2 * wide)
        weights[:, twice] = repeat_blocks(weight_form(x_ref[8:16, columns]))
        targets[:, columns] = target_form(x_ref[0:8, columns])
        return 0

    def turn(at, _):
        for part in range(LEAVES_SELF):
            columns = pl.ds(pl.multiple_of((at * LEAVES_SELF + part) * leaf, leaf), leaf)
            twice = pl.ds(pl.multiple_of((at * LEAVES_SELF + part) * 2 * leaf, leaf), 2 * leaf)
            self_ref[:, columns] = fold(kernel_term(sources[:, columns].T, targets[:, columns], weights[:, twice]))
        return 0

    lax.fori_loop(0, points // wide, prepare, 0)
    lax.fori_loop(0, points // (leaf * LEAVES_SELF), turn, 0)
    total = jnp.zeros((8, rank), F32)
    for at in range(chunks):
        x_high, x_low = two_pieces(x_ref[8:16, at * chunk:(at + 1) * chunk])
        left = jnp.concatenate([x_high, x_low], axis=0).astype(BF16)
        copies[at].wait()
        p_high, p_low = two_pieces(held[at])
        both = jnp.dot(left, p_high.astype(BF16), preferred_element_type=F32)
        part = jnp.dot(left, p_low.astype(BF16), preferred_element_type=F32)
        total += both[:8] + both[8:] + part[:8]
    for copy in range(node_ref.shape[0]):
        node_ref[copy, 8:16, :] = total


def first_step(copies, leaf, extended, projection, skel_index):
    points, rank = projection.shape
    chunks = 8
    return pl.pallas_call(
        functools.partial(first_kernel, leaf),
        out_shape=(
            jax.ShapeDtypeStruct((copies, 16, rank), F32),
            jax.ShapeDtypeStruct((8, points), F32),
        ),
        in_specs=[VMEM_SPEC, HBM_SPEC, VMEM_SPEC],
        out_specs=(VMEM_SPEC, VMEM_SPEC),
        scratch_shapes=[
            pltpu.VMEM((chunks, points // chunks, rank), F32),
            pltpu.VMEM((48, points), BF16),
            pltpu.VMEM((16, 2 * points), BF16),
            pltpu.VMEM((48, points), BF16),
            pltpu.SemaphoreType.DMA((chunks,)),
        ],
        compiler_params=pltpu.CompilerParams(vmem_limit_bytes=50 * 2**20),
        name="first_step",
    )(extended, projection, skel_index)


def climb(source, first, count, selection, rows, transfer, target, offset):
    rank = transfer[0].shape[1]
    t_high, t_low = transfer
    joined = jnp.concatenate(
        [
            jnp.concatenate([source[first + 2 * m + side, 8:16, :] for m in range(count)], axis=0)
            for side in range(2)
        ],
        axis=1,
    )
    high, low = two_pieces(joined)
    left = jnp.concatenate([high, low], axis=0).astype(BF16)
    both = jnp.dot(left, t_high, preferred_element_type=F32)
    part = jnp.dot(left, t_low, preferred_element_type=F32)
    moved = both[:8 * count] + both[8 * count:] + part[:8 * count]
    for m in range(count):
        target[offset + m, 8:16, :] = moved[m * 8:(m + 1) * 8, :]
        pieces = [
            source[first + 2 * m + side, 0:8, at * LANES:(at + 1) * LANES]
            for side in range(2)
            for at in range(rank // LANES)
        ]
        picked = selection[pl.ds(rows + m, 1), :]
        for half in range(rank // LANES):
            lanes = slice(half * LANES, (half + 1) * LANES)
            target[offset + m, 0:8, lanes] = pick_columns(pieces, picked[:, lanes])


def split_transfer(transfer_ref):
    t_high, t_low = two_pieces(transfer_ref[...])
    return t_high.astype(BF16), t_low.astype(BF16)


def near_kernel(near_ref, count_ref, self_ref, chip_ref, own_ref, other_ref, out_ref, sources, weights, targets, unpacked):
    leaves, slots = near_ref.shape
    points = own_ref.shape[1]
    leaf = points // leaves
    own_index = lax.axis_index("leaf")
    even = own_index % 2 == 0
    first_leaf = own_index * leaves
    wide = 16 * leaf
    empty = 3 * points
    sources[:, empty:] = jnp.zeros((48, leaf), BF16)
    weights[:, 2 * empty:] = jnp.zeros((16, 2 * leaf), BF16)

    front, parts = packed_parts(points)
    last = 3 * (points // 4)
    unpacked[0:6, 0:last] = other_ref[0:6, front]
    for part, columns in enumerate(parts):
        unpacked[2 * part:2 * part + 2, last:] = other_ref[6:8, columns]
    add_norm(unpacked)

    def prepare(at, _):
        columns = pl.ds(pl.multiple_of(at * wide, wide), wide)
        for part, (coords, values) in enumerate(
            ((chip_ref, chip_ref.at[pl.ds(8, 8)]), (own_ref, own_ref.at[pl.ds(8, 8)]), (unpacked, other_ref))
        ):
            window = pl.ds(pl.multiple_of(part * points + at * wide, wide), wide)
            sources[:, window] = source_form(coords[0:8, columns])
            twice = pl.ds(pl.multiple_of(2 * (part * points + at * wide), wide), 2 * wide)
            weights[:, twice] = repeat_blocks(weight_form(values[0:8, columns]))
        targets[:, columns] = target_form(own_ref[0:8, columns])
        return 0

    lax.fori_loop(0, points // wide, prepare, 0)

    def window_place(offset):
        below, above = offset < 0, offset >= leaves
        left = jnp.where(even, 2, 0)
        part = jnp.where(below, left, jnp.where(above, 2 - left, 1))
        local = jnp.where(below, offset + leaves, jnp.where(above, offset - leaves, offset))
        return part * leaves + jnp.clip(local, 0, leaves - 1)

    def one_leaf(at, live_slots):
        columns = pl.ds(pl.multiple_of(at * leaf, leaf), leaf)
        target = targets[:, columns]
        held, pieces = [], []
        for slot in range(1, live_slots):
            place = window_place(near_ref[at, slot] - first_leaf)
            place = jnp.where(slot < count_ref[at], place, 3 * leaves)
            window = pl.ds(pl.multiple_of(place * leaf, leaf), leaf)
            weight = weights[:, pl.ds(pl.multiple_of(place * 2 * leaf, leaf), 2 * leaf)]
            held.append(weight)
            pieces += kernel_pieces(sources[:, window].T, target, LANES, LANES)
        out_ref[:, columns] = self_ref[:, columns] + weigh(held, pieces)

    def turn(at, _):
        most = count_ref[NEAR_TURN * at]
        for leaf_at in range(1, NEAR_TURN):
            most = jnp.maximum(most, count_ref[NEAR_TURN * at + leaf_at])
        heavy = most > slots // 2

        @pl.when(heavy)
        def _():
            for leaf_at in range(NEAR_TURN):
                one_leaf(NEAR_TURN * at + leaf_at, slots)

        @pl.when(jnp.logical_not(heavy))
        def _():
            for leaf_at in range(NEAR_TURN):
                one_leaf(NEAR_TURN * at + leaf_at, slots // 2)

        return 0

    lax.fori_loop(0, leaves // NEAR_TURN, turn, 0)


def near_term(near_leaf, near_count, own_part, chip, own, other):
    leaves, slots = near_leaf.shape
    points = own.shape[1]
    entries = leaves * slots * (points // leaves) ** 2
    return pl.pallas_call(
        near_kernel,
        out_shape=jax.ShapeDtypeStruct((8, points), F32),
        in_specs=[SMEM_SPEC] * 2 + [VMEM_SPEC] * 4,
        out_specs=VMEM_SPEC,
        scratch_shapes=[
            pltpu.VMEM((48, 3 * points + points // leaves), BF16),
            pltpu.VMEM((16, 6 * points + 2 * (points // leaves)), BF16),
            pltpu.VMEM((48, points), BF16),
            pltpu.VMEM((8, points), F32),
        ],
        cost_estimate=pl.CostEstimate(flops=1000 * entries, bytes_accessed=4 * 64 * points, transcendentals=entries),
        compiler_params=pltpu.CompilerParams(vmem_limit_bytes=32 * 2**20),
        name="near_term",
    )(near_leaf, near_count, own_part, chip, own, other)


def far_kernel(scale, tile, own_ref, near_ref, gathered_ref, selection_ref, transfer_ref, out_ref, nodes, sources, weights):
    devices = gathered_ref.shape[0]
    levels = devices.bit_length() - 1
    own_index = lax.axis_index("leaf")
    transfer = split_transfer(transfer_ref)
    rank = transfer_ref.shape[1]
    held, first = gathered_ref, 0
    for level in range(levels):
        node = held[first + ((own_index >> level) ^ 1)]
        form = source_form(node[0:8])
        sources[level] = jnp.concatenate([form, jnp.zeros((LANES - 48, rank), BF16)], axis=0).T
        form = weight_form(node[8:16])
        weights[level] = jnp.concatenate([form, form], axis=1)
        if level < levels - 1:
            rows = devices - (devices >> level)
            climb(held, first, devices >> (level + 1), selection_ref, rows, transfer, nodes, rows)
            held, first = nodes, rows

    def turn(at, _):
        for part in range(FAR_TURN):
            columns = pl.ds(pl.multiple_of((at * FAR_TURN + part) * tile, tile), tile)
            target = target_form(own_ref[0:8, columns])
            target = jnp.concatenate([target, jnp.zeros((LANES - 48, tile), BF16)], axis=0)
            pieces = []
            for level in range(levels):
                pieces += kernel_pieces(sources[level], target, rank, rank)
            total = weigh([weights[level] for level in range(levels)], pieces)
            out_ref[:, columns] = (total + near_ref[:, columns]) * scale
        return 0

    lax.fori_loop(0, own_ref.shape[1] // (tile * FAR_TURN), turn, 0)


def far_term(scale, tile, own, near, gathered, selection, transfer):
    devices, _, rank = gathered.shape
    levels = devices.bit_length() - 1
    return pl.pallas_call(
        functools.partial(far_kernel, scale, tile),
        out_shape=jax.ShapeDtypeStruct((8, own.shape[1]), F32),
        in_specs=[VMEM_SPEC] * 5,
        out_specs=VMEM_SPEC,
        scratch_shapes=[
            pltpu.VMEM((devices - 2, 16, rank), F32),
            pltpu.VMEM((levels, rank, LANES), BF16),
            pltpu.VMEM((levels, 16, 2 * rank), BF16),
        ],
        compiler_params=pltpu.CompilerParams(vmem_limit_bytes=32 * 2**20),
        name="far_term",
    )(own, near, gathered, selection, transfer)


def body(coords, right_sides, projection, skel_index, selection, transfer, near_leaf, near_count):
    devices = lax.axis_size("leaf")
    leaves, slots = near_leaf.shape
    leaf = coords.shape[1] // leaves
    scale = 1.0 / (slots * leaf) ** 0.5
    extended, packed, skel_index = extend(coords, right_sides, skel_index)
    chip = swap(extended, "leaf", 0)
    other = swap(packed, "leaf", 1)
    node, own_part = first_step(devices, leaf, extended, projection, skel_index)
    gathered = lax.all_to_all(node, "leaf", 0, 0, tiled=True)
    near = near_term(near_leaf, near_count, own_part, chip, extended, other)
    return far_term(scale, leaf, extended, near, gathered, selection, transfer)


def solution(mesh):
    return jax.shard_map(
        body,
        mesh=mesh,
        in_specs=(
            P(None, "leaf"),
            P(None, "leaf"),
            P("leaf", None),
            P("leaf", None),
            P(),
            P(),
            P("leaf", None),
            P("leaf"),
        ),
        out_specs=P(None, "leaf"),
        check_vma=False,
    )
```
